32 devices in a mesh: seq: 2 (over x), ctx: 4 (over z), fsdp: 4 (over y, core).
Axes of the slice: x: 2, y: 2, z: 4, core: 2. Of those that a mesh axis runs over, the one named last changes fastest.
Arguments:
- hidden: bfloat16 [8, 1024, 1024], P(('seq', 'fsdp'), 'ctx'), may hold values from -6 to 6
- encoder: bfloat16 [8, 256, 1024], P(('seq', 'fsdp'), 'ctx'), may hold values from -6 to 6
- attn_qkv: bfloat16 [1024, 3072], P('fsdp'), may hold values from -0.1875 to 0.1875
- attn_out: bfloat16 [1024, 1024], P('fsdp'), may hold values from -0.5 to 0.5
- cross_q: bfloat16 [1024, 1024], P('fsdp'), may hold values from -0.1875 to 0.1875
- cross_kv: bfloat16 [1024, 2048], P('fsdp'), may hold values from -0.1875 to 0.1875
- cross_out: bfloat16 [1024, 1024], P('fsdp'), may hold values from -0.5 to 0.5
- ff_in: bfloat16 [1024, 4096], P('fsdp'), may hold values from -0.1875 to 0.1875
- ff_out: bfloat16 [4096, 1024], P('fsdp'), may hold values from -0.09375 to 0.09375
- norm_gains: bfloat16 [3, 1024], P(None, 'fsdp'), may hold values from 0.5 to 1.5
- norm_biases: bfloat16 [3, 1024], P(None, 'fsdp'), may hold values from -3 to 3
- block_table: int32 [4, 2], replicated, may hold values from 0 to 7, as said below
- out_grad: bfloat16 [8, 1024, 1024], P(('seq', 'fsdp'), 'ctx'), may hold values from -6 to 6
Outputs:
- mixed: bfloat16 [8, 1024, 1024], P(('seq', 'fsdp'), 'ctx')
- grad_input: float32 [8, 1024, 1024], P(('seq', 'fsdp'), 'ctx')
- grad_encoder: float32 [8, 256, 1024], P(('seq', 'fsdp'), 'ctx')
- grad_attn_qkv: float32 [1024, 3072], P('fsdp')
- grad_attn_out: float32 [1024, 1024], P('fsdp')
- grad_cross_q: float32 [1024, 1024], P('fsdp')
- grad_cross_kv: float32 [1024, 2048], P('fsdp')
- grad_cross_out: float32 [1024, 1024], P('fsdp')
- grad_ff_in: float32 [1024, 4096], P('fsdp')
- grad_ff_out: float32 [4096, 1024], P('fsdp')
- grad_norm_gains: float32 [3, 1024], P(None, 'fsdp')
- grad_norm_biases: float32 [3, 1024], P(None, 'fsdp')
The draws below stay inside these ranges and needn't reach their ends.
Inputs may be any that keep to these rules, and one draw needn't show every extreme that they name: `block_table`: row c holds two blocks b and 7 - b in either order; every block number of one sequence appears exactly once in the table.
All inputs are finite; a program needn't handle non-finite values.
Results may differ from the reference program's by a relative error of at most 0.023.
Values may be sent and summed in bfloat16 or wider, within the bound.
No kernel may reach another device: no remote copies, remote signals or barrier semaphores. Data moves between devices by JAX's collectives and lax.ppermute only.
A program may use at most 256 MiB of HBM per device.

```python
import math
import jax
import jax.numpy as jnp
from jax import lax

D = 1024
HEADS = 16
HEAD_DIM = 64
FF = 4096
BLK = 128
LEN = 1024
ENC = 256
SEQUENCES = 8
N_CTX = 4


def draw_block_table(key, part):
    key = jax.random.fold_in(key, 7)
    order = jax.random.permutation(jax.random.fold_in(key, 1), N_CTX).astype(jnp.int32)
    flips = jax.random.randint(jax.random.fold_in(key, 2), (N_CTX,), 0, 2).astype(jnp.int32)
    first = jnp.where(flips == 1, 2 * N_CTX - 1 - order, order)
    second = 2 * N_CTX - 1 - first
    return jnp.stack([first, second], axis=1).astype(jnp.int32)


def levels(key, shape, pieces, low, high):
    level, own = 1.0, jax.random.fold_in(key, 6)
    for axis_at, parts in pieces:
        heights = jnp.exp(jax.random.uniform(jax.random.fold_in(own, axis_at), (parts,), jnp.float32, low / len(pieces), high / len(pieces)))
        level = level * jnp.repeat(heights, shape[axis_at] // parts).reshape([-1 if axis == axis_at else 1 for axis in range(len(shape))])
    return level


def bell_draw(stream_key, shape, scale, reach, cuts=(), held_as=jnp.bfloat16):
    entries = scale * jax.random.normal(stream_key, shape, jnp.float32)
    if cuts:
        entries = entries * levels(stream_key, shape, cuts, -0.22, 0.18)
    return jnp.clip(entries, -reach, reach).astype(held_as)


def setup_inputs(seed: int = 0) -> dict:
    key_list = jax.random.split(jax.random.key(seed), 14)
    hidden = bell_draw(key_list[0], (SEQUENCES, LEN, D), 1.0, 6.0, ((0, 8), (1, 4)))
    encoder = bell_draw(key_list[1], (SEQUENCES, ENC, D), 1.0, 6.0, ((0, 8), (1, 4)))
    attn_qkv = bell_draw(key_list[2], (D, 3 * D), D ** -0.5, 0.1875, ((0, 4),))
    attn_out = bell_draw(key_list[3], (D, D), (D // 8) ** -0.5, 0.5, ((0, 4),))
    cross_q = bell_draw(key_list[4], (D, D), D ** -0.5, 0.1875, ((0, 4),))
    cross_kv = bell_draw(key_list[5], (D, 2 * D), D ** -0.5, 0.1875, ((0, 4),))
    cross_out = bell_draw(key_list[6], (D, D), (D // 8) ** -0.5, 0.5, ((0, 4),))
    ff_in = bell_draw(key_list[7], (D, FF), D ** -0.5, 0.1875, ((0, 4),))
    ff_out = bell_draw(key_list[8], (FF, D), FF ** -0.5, 0.09375, ((0, 4),))
    norm_gains = jnp.clip(1.0 + 0.1 * jax.random.normal(key_list[9], (3, D), jnp.float32), 0.5, 1.5).astype(jnp.bfloat16)
    norm_biases = bell_draw(key_list[10], (3, D), 0.5, 3.0, ((1, 4),))
    block_table = draw_block_table(jax.random.fold_in(key_list[13], 71), 0)
    out_grad = bell_draw(key_list[12], (SEQUENCES, LEN, D), 1.0, 6.0, ((0, 8), (1, 4)))
    return dict(hidden=hidden, encoder=encoder, attn_qkv=attn_qkv, attn_out=attn_out, cross_q=cross_q, cross_kv=cross_kv, cross_out=cross_out, ff_in=ff_in, ff_out=ff_out, norm_gains=norm_gains, norm_biases=norm_biases, block_table=block_table, out_grad=out_grad)


@jax.custom_vjp
def low(v):
    return lax.optimization_barrier(v.astype(jnp.bfloat16)).astype(jnp.float32)

@jax.custom_vjp
def low_back(v):
    return v

def low_keep(v):
    return (low(v), None)

def low_pass(kept, grad):
    return (grad,)

def back_keep(v):
    return (v, None)

def back_low(kept, grad):
    return (low(grad),)
low.defvjp(low_keep, low_pass)
low_back.defvjp(back_keep, back_low)

def dense(left, right):
    return jnp.dot(left, right, precision=lax.Precision.HIGHEST)

def layer_norm(value, gain, shift):
    centre = lax.optimization_barrier(jnp.mean(value, -1, keepdims=True))
    centred = value - centre
    spread = lax.optimization_barrier(jnp.mean(centred * centred, -1, keepdims=True))
    return centred * lax.rsqrt(spread + 1e-05) * gain + shift

def attend(query, keys, values, query_pos, key_pos):
    rows = query.shape[0]
    size = math.gcd(rows, 512)
    count = rows // size
    causal = query_pos is not None
    places = query_pos if causal else jnp.zeros((rows,), jnp.int32)

    def block(item):
        part, where_at = item
        scores = low_back(jnp.einsum('qhd,khd->hqk', part, keys, precision=lax.Precision.HIGHEST) * HEAD_DIM ** (-0.5))
        if causal:
            scores = jnp.where(key_pos[None, None, :] <= where_at[None, :, None], scores, -1e+30)
        probs = low(jax.nn.softmax(scores, axis=-1))
        return jnp.einsum('hqk,khd->qhd', probs, values, precision=lax.Precision.HIGHEST)
    out = lax.map(jax.checkpoint(block), (query.reshape(count, size, HEADS, HEAD_DIM), places.reshape(count, size)))
    return out.reshape(rows, HEADS * HEAD_DIM)

def split(block_value):
    return block_value.reshape(block_value.shape[0], HEADS, HEAD_DIM)

def layer(inputs, states, params, positions):
    wqkv, wout_self, wcq, wckv, wco, wfin, wfout, gains, shifts = params
    width = inputs.shape[1]
    qkv = low(low_back(dense(inputs, wqkv)))
    att = low(low_back(attend(split(qkv[:, :width]), split(qkv[:, width:2 * width]), split(qkv[:, 2 * width:]), positions, positions)))
    first = layer_norm(inputs + low_back(dense(att, wout_self)), gains[0], shifts[0])
    cross_query = low(low_back(dense(low(first), wcq)))
    enc_kv = low(low_back(dense(states, wckv)))
    cat = low(low_back(attend(split(cross_query), split(enc_kv[:, :width]), split(enc_kv[:, width:]), None, None)))
    second = layer_norm(first + low_back(dense(cat, wco)), gains[1], shifts[1])
    pre = low_back(dense(low(second), wfin))
    act = low(jax.nn.gelu(pre, approximate=False))
    return layer_norm(second + low_back(dense(act, wfout)), gains[2], shifts[2])

def reference(hidden, encoder, attn_qkv, attn_out, cross_q, cross_kv, cross_out, ff_in, ff_out, norm_gains, norm_biases, block_table, out_grad):
    params = tuple((matrix.astype(jnp.float32) for matrix in (attn_qkv, attn_out, cross_q, cross_kv, cross_out, ff_in, ff_out, norm_gains, norm_biases)))
    positions = (block_table[:, :, None] * BLK + jnp.arange(BLK, dtype=jnp.int32)[None, None, :]).reshape(-1).astype(jnp.int32)

    def one(totals, item):
        source, memory, cotangent = item
        result, pull = jax.vjp(lambda inputs, states, *weights: layer(inputs, states, weights, positions), source.astype(jnp.float32), memory.astype(jnp.float32), *params)
        grads = pull(cotangent.astype(jnp.float32))
        totals = tuple((total + grad for total, grad in zip(totals, grads[2:])))
        return (totals, (result.astype(jnp.bfloat16), grads[0], grads[1]))
    start = tuple((jnp.zeros(param.shape, jnp.float32) for param in params))
    totals, (mixed, grad_input, grad_encoder) = lax.scan(one, start, (hidden, encoder, out_grad))
    return (mixed, grad_input, grad_encoder, totals[0], totals[1], totals[2], totals[3], totals[4], totals[5], totals[6], totals[7], totals[8])
```

```python
import functools

import jax
import jax.numpy as jnp
from jax import lax
from jax.experimental import pallas as pl
from jax.experimental.pallas import tpu as pltpu
from jax.sharding import PartitionSpec as P

HEADS = 16
HEAD_DIM = 64
TILE = 256
GROUP = 4
VMEM_LIMIT = 48 * 1024 * 1024
BF = jnp.bfloat16
F32 = jnp.float32
SMEM = pl.BlockSpec(memory_space=pltpu.SMEM)


def dot(left, right):
    return jnp.dot(left, right, preferred_element_type=F32)


def dot_rows(left, right):
    return lax.dot_general(left, right, (((0,), (0,)), ((), ())), preferred_element_type=F32)


def dot_cols(left, right):
    return lax.dot_general(left, right, (((1,), (1,)), ((), ())), preferred_element_type=F32)


def after(value, *others):
    return lax.optimization_barrier((value, *others))[0]


def causal_mask(tile):
    key = lax.broadcasted_iota(jnp.int32, (tile, tile), 0)
    query = lax.broadcasted_iota(jnp.int32, (tile, tile), 1)
    return key <= query


def lanes_of(heads):
    return [slice(head * HEAD_DIM, (head + 1) * HEAD_DIM) for head in range(heads)]


def joined_heads(values, axis):
    return values[0] if len(values) == 1 else jnp.concatenate(values, axis)


def spans(causal, at, keys):
    if not causal:
        return [(0, keys, False)]
    return ([(0, at * TILE, False)] if at else []) + [(at * TILE, TILE, True)]


def attend_kernel(causal, heads, steps, q_ref, k_ref, v_ref, out_ref, out_t_ref, lse_ref):
    query = q_ref[...] * HEAD_DIM**-0.5
    lanes = lanes_of(heads)

    def finish(outs):
        out_t = joined_heads(outs, 0)
        out_t_ref[...] = out_t
        out_ref[...] = out_t.T.astype(BF)

    def whole(at):
        parts = spans(causal, at, k_ref.shape[0])
        outs = []
        for head, lane in enumerate(lanes):
            scores = []
            for start, size, masked in parts:
                score = dot_cols(k_ref[start : start + size, lane], query[:, lane])
                scores.append(jnp.where(causal_mask(TILE), score, -1e30) if masked else score)
            top = functools.reduce(jnp.maximum, [jnp.max(score, 0, keepdims=True) for score in scores])
            probs = [jnp.exp(score - top) for score in scores]
            total = sum(jnp.sum(prob, 0, keepdims=True) for prob in probs)
            accum = sum(
                dot_rows(v_ref[start : start + size, lane], prob.astype(BF))
                for (start, size, _), prob in zip(parts, probs)
            )
            outs.append(accum / total)
            lse_ref[head : head + 1, :] = top + jnp.log(total)
        finish(outs)

    def rolled(at):
        def step(index, carry, masked):
            span = pl.ds(pl.multiple_of(index * TILE, TILE), TILE)
            keys, values = k_ref[span, :], v_ref[span, :]
            after_step = []
            for head, lane in enumerate(lanes):
                top, total, accum = carry[head]
                score = dot_cols(keys[:, lane], query[:, lane])
                if masked:
                    score = jnp.where(causal_mask(TILE), score, -1e30)
                new_top = jnp.maximum(top, jnp.max(score, 0, keepdims=True))
                prob = jnp.exp(score - new_top)
                decay = jnp.exp(top - new_top)
                total = total * decay + jnp.sum(prob, 0, keepdims=True)
                accum = accum * decay + dot_rows(values[:, lane], prob.astype(BF))
                after_step.append((new_top, total, accum))
            return tuple(after_step)

        rows = query.shape[0]
        carry = tuple(
            (
                jnp.full((1, rows), -1e30, F32),
                jnp.zeros((1, rows), F32),
                jnp.zeros((HEAD_DIM, rows), F32),
            )
            for _ in lanes
        )
        carry = lax.fori_loop(0, at, functools.partial(step, masked=False), carry)
        carry = step(at, carry, True)
        for head in range(heads):
            lse_ref[head : head + 1, :] = carry[head][0] + jnp.log(carry[head][1])
        finish([accum / total for _, total, accum in carry])

    run_tiles(causal, steps, whole, rolled)


def run_tiles(causal, steps, whole, rolled):
    at = pl.program_id(1)
    if not causal:
        whole(0)
    elif steps <= 4:
        for tile in range(steps):
            pl.when(at == tile)(functools.partial(whole, tile))
    else:
        rolled(at)


def attend_back_kernel(
    causal, heads, steps, q_ref, k_ref, v_ref, do_ref, out_t_ref, lse_ref,
    dq_ref, dk_ref, dv_ref, dk_sum, dv_sum,
):
    query = q_ref[...] * HEAD_DIM**-0.5
    d_out = do_ref[...]
    lanes = lanes_of(heads)
    weighed = d_out.astype(F32).T * out_t_ref[...]
    deltas = [jnp.sum(weighed[lane, :], 0, keepdims=True) for lane in lanes]
    totals = [lse_ref[head : head + 1, :] for head in range(heads)]

    @pl.when(pl.program_id(1) == 0)
    def _():
        dk_sum[...] = jnp.zeros_like(dk_sum)
        dv_sum[...] = jnp.zeros_like(dv_sum)

    def part(span, masked, d_query):
        keys, values = k_ref[span, :], v_ref[span, :]
        d_keys, d_values, out = [], [], []
        for head, lane in enumerate(lanes):
            score = dot_cols(keys[:, lane], query[:, lane])
            prob = jnp.exp(score - totals[head])
            if masked:
                prob = jnp.where(causal_mask(TILE), prob, 0.0)
            d_prob = dot_cols(values[:, lane], d_out[:, lane])
            d_score = (prob * (d_prob - deltas[head])).astype(BF)
            d_values.append(dot(prob.astype(BF), d_out[:, lane]))
            d_keys.append(dot(d_score, query[:, lane]))
            out.append(d_query[head] + dot_rows(keys[:, lane], d_score))
        dk_sum[span, :] += joined_heads(d_keys, 1)
        dv_sum[span, :] += joined_heads(d_values, 1)
        return tuple(out)

    start = tuple(jnp.zeros((HEAD_DIM, query.shape[0]), F32) for _ in lanes)

    def finish(d_query):
        dq_ref[...] = (joined_heads(d_query, 0).T * HEAD_DIM**-0.5).astype(BF)

    def whole(at):
        d_query = start
        for first, size, masked in spans(causal, at, k_ref.shape[0]):
            d_query = part(slice(first, first + size), masked, d_query)
        finish(d_query)

    def rolled(at):
        def step(index, carry):
            return part(pl.ds(pl.multiple_of(index * TILE, TILE), TILE), False, carry)

        d_query = lax.fori_loop(0, at, step, start)
        finish(part(pl.ds(pl.multiple_of(at * TILE, TILE), TILE), True, d_query))

    run_tiles(causal, steps, whole, rolled)

    @pl.when(pl.program_id(1) == steps - 1)
    def _():
        dk_ref[...] = dk_sum[...].astype(BF)
        dv_ref[...] = dv_sum[...].astype(BF)


def attend_specs(rows, keys, width, parts):
    group = min(width, GROUP * HEAD_DIM)
    groups = width // group

    def tall(part):
        return pl.BlockSpec((keys, group), lambda g, i: (0, part * groups + g))

    def query(part):
        return pl.BlockSpec((TILE, group), lambda g, i: (i, part * groups + g))

    return (
        (groups, rows // TILE), group, query(0), tall(parts[0]), tall(parts[1]), tall(0),
        pl.BlockSpec((group, TILE), lambda g, i: (g, i)),
        pl.BlockSpec((8, TILE), lambda g, i: (g, i)),
    )


def attend(causal, query, keys, values, width, parts):
    rows, depth = query.shape[0], keys.shape[0]
    grid, group, q_spec, k_spec, v_spec, _, t_spec, lse_spec = attend_specs(rows, depth, width, parts)
    return pl.pallas_call(
        functools.partial(attend_kernel, causal, group // HEAD_DIM, grid[1]),
        grid=grid,
        in_specs=[q_spec, k_spec, v_spec],
        out_specs=[q_spec, t_spec, lse_spec],
        out_shape=[
            jax.ShapeDtypeStruct((rows, width), BF),
            jax.ShapeDtypeStruct((width, rows), F32),
            jax.ShapeDtypeStruct((8 * grid[0], rows), F32),
        ],
        compiler_params=pltpu.CompilerParams(vmem_limit_bytes=VMEM_LIMIT),
        cost_estimate=pl.CostEstimate(
            flops=4 * rows * depth * width, bytes_accessed=8 * (rows + depth) * width,
            transcendentals=rows * depth * width // HEAD_DIM,
        ),
    )(query, keys, values)


def attend_back(causal, query, keys, values, d_out, out_t, lse, width, parts):
    rows, depth = query.shape[0], keys.shape[0]
    grid, group, q_spec, k_spec, v_spec, tall, t_spec, lse_spec = attend_specs(rows, depth, width, parts)
    return pl.pallas_call(
        functools.partial(attend_back_kernel, causal, group // HEAD_DIM, grid[1]),
        grid=grid,
        in_specs=[q_spec, k_spec, v_spec, q_spec, t_spec, lse_spec],
        out_specs=[q_spec, tall, tall],
        out_shape=[
            jax.ShapeDtypeStruct((rows, width), BF),
            jax.ShapeDtypeStruct((depth, width), BF),
            jax.ShapeDtypeStruct((depth, width), BF),
        ],
        scratch_shapes=[pltpu.VMEM((depth, group), F32), pltpu.VMEM((depth, group), F32)],
        compiler_params=pltpu.CompilerParams(vmem_limit_bytes=VMEM_LIMIT),
        cost_estimate=pl.CostEstimate(
            flops=10 * rows * depth * width, bytes_accessed=12 * (rows + depth) * width,
            transcendentals=rows * depth * width // HEAD_DIM,
        ),
    )(query, keys, values, d_out, out_t, lse)


IN_VMEM = pl.BlockSpec(memory_space=pltpu.VMEM)


def moved(kernel, scalars, values, out_shapes, dtype=BF):
    size = sum(value.size * value.dtype.itemsize for value in values)
    return pl.pallas_call(
        kernel,
        in_specs=[SMEM] * len(scalars) + [IN_VMEM] * len(values),
        out_specs=[IN_VMEM] * len(out_shapes),
        out_shape=[jax.ShapeDtypeStruct(shape, dtype) for shape in out_shapes],
        compiler_params=pltpu.CompilerParams(vmem_limit_bytes=VMEM_LIMIT),
        cost_estimate=pl.CostEstimate(flops=0, bytes_accessed=2 * size, transcendentals=0),
    )(*scalars, *values)


def place(rows, pieces, starts, *scalars):
    def kernel(*refs):
        values, out_ref = refs[len(scalars) : -1], refs[-1]
        for start, value in zip(starts(*refs[: len(scalars)]), values):
            out_ref[pl.ds(pl.multiple_of(start, 16), value.shape[0]), :] = value[...]

    return moved(kernel, scalars, pieces, [(rows, pieces[0].shape[1])])[0]


def cut(value, rows, count, starts, *scalars):
    def kernel(*refs):
        source, outs = refs[len(scalars)], refs[len(scalars) + 1 :]
        first = starts(*refs[: len(scalars)])
        size = rows // 2
        for index, start in enumerate(first):
            outs[index // 2][index % 2 * size : (index % 2 + 1) * size, :] = source[
                pl.ds(pl.multiple_of(start, 16), size), :
            ]

    return moved(kernel, scalars, [value], [(rows, value.shape[1])] * count)


def line_up(pieces, parts, at, dtype=BF):
    rows, columns = pieces[0].shape
    size = columns // parts

    def kernel(at_ref, *refs):
        values, out_ref = refs[:-1], refs[-1]
        for mask, value in enumerate(values):
            owner = at_ref[0] ^ mask
            for part in range(parts):
                start = part * size * len(values) + owner * size
                out_ref[:, pl.ds(pl.multiple_of(start, 128), size)] = value[
                    :, part * size : (part + 1) * size
                ].astype(dtype)

    return moved(kernel, [at], pieces, [(rows, columns * len(pieces))], dtype)[0]


def turn(value, starts, *scalars):
    def kernel(*refs):
        source, out_ref = refs[len(scalars) :]
        first = starts(*refs[: len(scalars)])
        size = source.shape[1] // len(first)
        for index, start in enumerate(first):
            out_ref[:, index * size : (index + 1) * size] = source[
                :, pl.ds(pl.multiple_of(start, 128), size)
            ]

    return moved(kernel, scalars, [value], [value.shape])[0]


def two_halves(kernel, own, other, at, out_widths):
    rows = out_widths[0][0]

    def body(at_ref, own_ref, other_ref, *outs):
        here = pl.program_id(0) == at_ref[0]
        pl.when(here)(lambda: kernel(own_ref, *outs))
        pl.when(jnp.logical_not(here))(lambda: kernel(other_ref, *outs))

    whole = pl.BlockSpec(own.shape, lambda i: (0, 0))
    return pl.pallas_call(
        body,
        grid=(2,),
        in_specs=[SMEM, whole, whole],
        out_specs=[pl.BlockSpec((rows, width), lambda i: (i, 0)) for _, width in out_widths],
        out_shape=[jax.ShapeDtypeStruct((2 * rows, width), F32) for _, width in out_widths],
        compiler_params=pltpu.CompilerParams(vmem_limit_bytes=VMEM_LIMIT),
        cost_estimate=pl.CostEstimate(flops=0, bytes_accessed=12 * own.size, transcendentals=0),
    )(at, own, other)


def split_columns_kernel(widths, source, *outs):
    at = 0
    for width, out in zip(widths, outs):
        out[...] = source[:, at : at + width].astype(F32)
        at += width


def spread_parts_kernel(owners, parts, source, out):
    rows, size = out.shape[0], source.shape[1] // parts
    width = out.shape[1] // parts
    for owner in range(owners):
        for part in range(parts):
            out[:, part * width + owner * size : part * width + (owner + 1) * size] = source[
                owner * rows : (owner + 1) * rows, part * size : (part + 1) * size
            ].astype(F32)


def norm_parts(value):
    centre = jnp.mean(value, -1, keepdims=True)
    centred = value - centre
    spread = jnp.mean(centred * centred, -1, keepdims=True)
    scale = lax.rsqrt(spread + 1e-05)
    return centred * scale, scale


def norm_back(grad, unit, scale, gain):
    slope = grad * gain
    d_value = scale * (
        slope
        - jnp.mean(slope, -1, keepdims=True)
        - unit * jnp.mean(slope * unit, -1, keepdims=True)
    )
    return d_value, jnp.sum(grad * unit, 0, keepdims=True), jnp.sum(grad, 0, keepdims=True)


def local(
    S, C, F,
    hidden, encoder, attn_qkv, attn_out, cross_q, cross_kv, cross_out, ff_in, ff_out,
    norm_gains, norm_biases, block_table, out_grad,
):
    rows, width = hidden.shape[1:]
    enc_rows = encoder.shape[1]
    half = rows // 2
    K = 2
    Y = F // K
    head_width = width // C
    ff_width = ff_in.shape[1] // F
    s, c, f = (lax.axis_index(name).astype(jnp.uint32) for name in ("seq", "ctx", "fsdp"))
    index_of = {"seq": s, "ctx": c, "fsdp": f}
    size_of = {"seq": S, "ctx": C, "fsdp": F}
    s_scalar, c_scalar, f_scalar = (index.astype(jnp.int32).reshape(1) for index in (s, c, f))

    def pick(value, index, axis=0):
        return lax.dynamic_index_in_dim(value, index, axis, keepdims=False)

    def bits_of(axis):
        return [1 << i for i in range(size_of[axis].bit_length() - 1)]

    def swap(value, axis, mask):
        return lax.ppermute(value, axis, [(i, i ^ mask) for i in range(size_of[axis])])

    def is_low(axis, bit):
        return (index_of[axis] & bit) == 0

    def give(parts, axis, bit):
        view = parts.reshape(parts.shape[0] // 2, 2, *parts.shape[1:])
        mine = (index_of[axis] // bit) & 1
        return pick(view, mine, 1), swap(pick(view, mine ^ 1, 1), axis, bit)

    def double(value, got, axis, bit):
        both = jnp.where(
            is_low(axis, bit), jnp.stack([value, got], 1), jnp.stack([got, value], 1)
        )
        return both.reshape(2 * value.shape[0], *value.shape[1:])

    def gather_over(value, axis):
        value = value[None]
        for bit in reversed(bits_of(axis)):
            value = double(value, swap(value, axis, bit), axis, bit)
        return value

    def by_owner_of(got, axis):
        stacked = jnp.stack(got)
        for bit in bits_of(axis):
            view = stacked.reshape(size_of[axis] // (2 * bit), 2, bit, *stacked.shape[1:])
            view = jnp.where(is_low(axis, bit), view, view[:, ::-1])
            stacked = view.reshape(stacked.shape)
        return stacked

    def exchanged(piece_of, axis):
        index = index_of[axis]
        return [piece_of(index)] + [
            swap(piece_of(index ^ mask), axis, mask) for mask in range(1, size_of[axis])
        ]

    def my_columns(weight, parts):
        size = weight.shape[1] // parts
        return jnp.concatenate(
            [
                lax.dynamic_slice_in_dim(weight, part * size + c * head_width, head_width, 1)
                for part in range(parts)
            ],
            1,
        )

    def to_rows(value):
        def starts(c_ref, table_ref):
            return [table_ref[c_ref[0] ^ mask, b] * half for mask in range(C) for b in range(2)]

        pieces = cut(value, rows, C, starts, c_scalar, block_table)
        return [pieces[0]] + [swap(pieces[mask], "ctx", mask) for mask in range(1, C)]

    def columns_in_order(got, parts):
        size = got[0].shape[1] // parts
        if size % 128 == 0:
            return line_up(got, parts, c_scalar)
        view = by_owner_of(got, "ctx").reshape(C, got[0].shape[0], parts, size)
        return view.transpose(1, 2, 0, 3).reshape(got[0].shape[0], C * parts * size)

    def to_columns(got):
        pieces = [value[b * half : (b + 1) * half] for value in got for b in range(2)]

        def starts(c_ref, table_ref):
            return [table_ref[c_ref[0] ^ mask, b] * half for mask in range(C) for b in range(2)]

        return place(C * rows, pieces, starts, c_scalar, block_table)

    def joined(lefts, rights):
        return dot_rows(jnp.concatenate(lefts, 0), jnp.concatenate(rights, 0)).astype(BF)

    flat = hidden.reshape(rows, width)
    enc = encoder.reshape(enc_rows, width)
    near = list(range(1, K))
    far = [mask for mask in range(F) if mask >= K]

    def near_first(size):
        return lambda f_ref: [(f_ref[0] ^ mask) * size for mask in range(F)]

    def spread(value):
        got = {mask: swap(value, "fsdp", mask) for mask in near}
        got.update({mask: swap(value, "fsdp", mask) for mask in far if mask % K == 0})
        return got

    def passed_on(got):
        return {mask: swap(got[mask - mask % K], "fsdp", mask % K) for mask in far if mask % K}

    slice_here = my_columns(attn_qkv, 3)
    norms = jnp.concatenate([norm_gains, norm_biases], 0)
    x_moving = [flat[:half], flat[half:]]
    x_pieces = list(x_moving)
    seen = []
    for step in range(C - 1):
        sent = {"x": [lax.ppermute(v, "ctx", [(i, (i + 1) % C) for i in range(C)]) for v in x_moving]}
        if step == 0:
            sent["slices"] = spread(slice_here)
            sent["norms"] = swap(norms, "fsdp", F // 2)
        sent = lax.optimization_barrier(sent)
        x_moving = sent["x"]
        x_pieces += x_moving
        seen.append(x_moving[0])
        if step == 0:
            slices, norms_got = sent["slices"], sent["norms"]
            slices.update(passed_on(slices))
            norms = double(norms[None], norms_got[None], "fsdp", F // 2)
            for bit in reversed(bits_of("fsdp")[:-1]):
                norms = double(norms, swap(norms, "fsdp", bit), "fsdp", bit)
    outs = spread(after(attn_out, seen[0]))
    outs.update(passed_on(outs))
    size = attn_qkv.shape[0]
    w_mine = place(width, [slice_here] + [slices[mask] for mask in near + far], near_first(size), f_scalar)
    w_out = place(width, [attn_out] + [outs[mask] for mask in near + far], near_first(size), f_scalar)
    norms = norms.astype(F32).transpose(1, 0, 2).reshape(6, width)
    gains, shifts = norms[:3], norms[3:]

    def x_starts(c_ref, table_ref):
        return [table_ref[(c_ref[0] + C - hop) & (C - 1), b] * half for hop in range(C) for b in range(2)]

    x_all = place(C * rows, x_pieces, x_starts, c_scalar, block_table)

    def gather(shard):
        return lax.all_gather(shard, "fsdp", axis=0, tiled=True)

    w_ckv = gather(cross_kv)
    w_cq, w_co = gather(after(cross_q, seen[0])), gather(after(cross_out, seen[0]))
    ff_later = after(ff_in, x_moving[0])
    ff_pieces = exchanged(
        lambda owner: lax.dynamic_slice_in_dim(ff_later, owner * ff_width, ff_width, 1), "fsdp"
    )
    w_ff = ff_out

    turns = [0]
    for bit in reversed(bits_of("fsdp")):
        turns = turns + [turn | bit for turn in turns]

    def turned(value):
        size = value.shape[1] // (F * S)
        if size % 128 == 0:
            return turn(
                value,
                lambda f_ref, s_ref: [
                    (f_ref[0] ^ mask) * (S * size) + (s_ref[0] ^ there) * size
                    for mask in turns
                    for there in range(S)
                ],
                f_scalar,
                s_scalar,
            )
        blocks = []
        for mask in turns:
            for there in range(S):
                at = (f ^ mask) * (S * size) + (s ^ there) * size
                blocks.append(lax.dynamic_slice_in_dim(value, at, size, 1))
        return jnp.concatenate(blocks, 1)

    class Tall:
        levels = [("fsdp", bit) for bit in bits_of("fsdp")] + [("seq", bit) for bit in bits_of("seq")]

        def __init__(self, left, right):
            self.left, self.right, self.got = left, right, []
            self.size = left.shape[1]
            self.at = 0

        def term(self, start, stop, token):
            right, got = self.right, self.got
            if token is not None:
                right, got = lax.optimization_barrier((right, got, token))[:2]
            total = dot_rows(self.left[:, start:stop], right)
            for value in got:
                total = total + value[start:stop].astype(F32)
            return total.astype(BF)

        def start(self, token=None, count=1):
            for _ in range(count):
                axis, bit = self.levels[self.at]
                self.at += 1
                self.size //= 2
                sent = self.term(self.size, 2 * self.size, token)
                self.got.append(swap(sent, axis, bit))
            return sent

        def end(self, token=None):
            return self.term(0, self.size, token)

    enc_all = after(enc, x_moving[0])[None]
    for bit in reversed(bits_of("ctx")):
        enc_some, enc_all = enc_all, double(enc_all, swap(enc_all, "ctx", bit), "ctx", bit)
    enc_all = enc_all.reshape(C * enc_rows, width)
    qkv = after(dot(x_all, w_mine).astype(BF), enc_some)
    if head_width % (2 * HEAD_DIM) == 0:
        self_in, self_parts = (qkv, qkv, qkv), (1, 2)
    else:
        self_in, self_parts = jnp.split(qkv, 3, 1), (0, 0)
    att_mine, att_t, att_lse = attend(True, *self_in, head_width, self_parts)
    att = columns_in_order(to_rows(att_mine), 1)
    ekv = dot(enc_all, w_ckv).astype(BF)
    w_in = place(width, ff_pieces, near_first(size), f_scalar)
    unit_0, scale_0 = norm_parts(flat.astype(F32) + dot(att, w_out))
    h_1 = unit_0 * gains[0] + shifts[0]
    h_1_low = h_1.astype(BF)

    cq = dot(h_1_low, w_cq).astype(BF)
    cat, cat_t, cat_lse = attend(False, cq, ekv, ekv, width, (0, 1))
    unit_1, scale_1 = norm_parts(h_1 + dot(cat, w_co))
    h_2 = unit_1 * gains[1] + shifts[1]
    h_2_low = h_2.astype(BF)

    def exchange(value, work, close):
        moving = {dy: swap(value, "fsdp", dy * K) for dy in range(1, Y)}

        def with_pair(there):
            return jnp.concatenate([there] + [swap(there, "fsdp", mask) for mask in near], 0)

        def pair_sum(term):
            view = term.astype(BF).reshape(K, -1, term.shape[1])
            total = view[0].astype(F32)
            for mask in near:
                total = total + swap(view[mask], "fsdp", mask).astype(F32)
            return total

        group = [with_pair(value)]
        worked = [work(0, group[0])]
        last = worked[0][0]
        for dy in range(1, Y):
            group.append(with_pair(after(moving[dy], last)))
            worked.append(work(dy, group[dy]))
            last = worked[dy][0]
        back, sent = [], None
        for dy in range(1, Y):
            sent = pair_sum(close(worked[dy])).astype(BF)
            back.append(swap(sent, "fsdp", dy * K))

        def finish(hold=()):
            own = worked[0] if sent is None else lax.optimization_barrier((worked[0], sent))[0]
            own = pair_sum(close(own))
            got = lax.optimization_barrier((back, own, hold))[0] if back else back
            return sum((value.astype(F32) for value in got), own)

        return group, worked, sent if back else last, finish

    def feed_forward(dy, value):
        pre = dot(value, w_in)
        cdf = 0.5 * (1.0 + lax.erf(pre * 0.5**0.5))
        slope = cdf + pre * (jnp.exp(-0.5 * pre * pre) * (2.0 * jnp.pi) ** -0.5)
        return lax.optimization_barrier(((pre * cdf).astype(BF), slope))

    h_2_rows, worked, _, finish = exchange(h_2_low, feed_forward, lambda got: dot(got[0], w_ff))
    acts, slopes = [got[0] for got in worked], [got[1] for got in worked]
    x_later, enc_later, w_out_later = (after(value, h_2_low) for value in (x_all, enc_all, w_out))
    x_turned, enc_turned = turned(x_later), turned(enc_later)
    cat_turned, h_1_turned, att_turned = turned(cat), turned(h_1_low), turned(after(att, h_2_low))
    w_out_turned = w_out_later.reshape(C, head_width, width)
    w_out_turned = [pick(w_out_turned, c ^ mask) for mask in range(C)]
    total = finish((x_turned, enc_turned, cat_turned, h_1_turned, att_turned, w_out_turned))
    unit_2, scale_2 = norm_parts(h_2 + total)

    grad = out_grad.reshape(rows, width).astype(F32)
    d_r3, d_gain_2, d_shift_2 = norm_back(grad, unit_2, scale_2, gains[2])

    def feed_back(dy, value):
        return ((dot_cols(value, w_ff) * slopes[dy]).astype(BF),)

    df_rows, worked, sent, finish = exchange(
        d_r3.astype(BF), feed_back, lambda got: dot_cols(got[0], w_in)
    )
    d_pres = [got[0] for got in worked]

    def by_owner(partial):
        return partial.astype(BF).reshape(F, -1, partial.shape[1])

    first_of = {axis: bits_of(axis)[:1] for axis in size_of}
    rest_of = {axis: bits_of(axis)[1:] for axis in size_of}

    class Sum:
        def __init__(self, parts, dtype=BF):
            self.value, self.pair, self.dtype = parts, None, dtype

        def start(self, axis, bits, token, kind="halve"):
            for at, bit in enumerate(bits):
                if at:
                    self.end()
                value = after(self.value, token)
                self.pair = give(value, axis, bit) if kind == "halve" else (value, swap(value, axis, bit))
                self.how = (kind, axis, bit)

        def end(self, token=None):
            if self.pair is None:
                return
            kept, got = self.pair
            self.pair = None
            if token is not None:
                got = after(got, token)
            if self.how[0] == "double":
                self.value = double(kept, got, *self.how[1:])
            else:
                self.value = (kept.astype(F32) + got.astype(F32)).astype(self.dtype)

        def shape(self, *shape):
            self.value = self.value.reshape(*shape)

    ctx_up, ctx_last = rest_of["ctx"][::-1], first_of["ctx"]
    seq_bits = bits_of("seq")

    tile_ff_in = joined([after(value, sent) for value in h_2_rows], d_pres)
    tile_ff_out = joined([after(act, sent) for act in acts], df_rows)
    tile_ff_in, tile_ff_out = lax.optimization_barrier((tile_ff_in, tile_ff_out))
    def turned_chunks(value):
        split = [2] * (C.bit_length() - 1)
        view = value.reshape(S, *split, *value.shape[1:])
        axes = (0, *range(len(split), 0, -1), len(split) + 1, len(split) + 2)
        return view.transpose(*axes).reshape(value.shape)

    tiles = jnp.concatenate(
        [
            turned_chunks(tile_ff_out.reshape(S * C, -1, width)),
            turned_chunks(
                tile_ff_in.reshape(F, S * C, -1, ff_width).transpose(1, 0, 2, 3).reshape(S * C, -1, width)
            ),
        ],
        1,
    )
    tile_rows = tiles.shape[1]
    d_h2 = d_r3 + finish((tiles,))

    def pair_sum_over(value, axis, bit):
        groups = [[i, i | bit] for i in range(size_of[axis]) if not i & bit]
        return lax.psum_scatter(value, axis, scatter_dimension=0, axis_index_groups=groups, tiled=True)

    part = pair_sum_over(tiles.reshape(-1, width), "seq", 1)

    qkv_shards = spread(after(attn_qkv, d_h2))
    d_r2, d_gain_1, d_shift_1 = norm_back(d_h2, unit_1, scale_1, gains[1])
    dc = d_r2.astype(BF)
    d_cat = dot_cols(dc, w_co).astype(BF)
    co = Tall(cat_turned, dc)
    token = co.start(d_cat)
    dcq, dek, dev = attend_back(False, cq, ekv, ekv, after(d_cat, token), cat_t, cat_lse, width, (0, 1))

    d_h1 = d_r2 + dot_cols(dcq, w_cq)
    d_r1, d_gain_0, d_shift_0 = norm_back(d_h1, unit_0, scale_0, gains[0])
    da = d_r1.astype(BF)
    d_att_pieces = [dot_cols(da, piece).astype(BF) for piece in w_out_turned]

    d_att_got = [d_att_pieces[0]] + [swap(d_att_pieces[mask], "ctx", mask) for mask in range(1, C)]
    t3 = (d_att_pieces, d_att_got[1] if C > 1 else ())
    fsdp_rest = len(rest_of["fsdp"])
    norm_terms = jnp.concatenate([d_gain_0, d_gain_1, d_gain_2, d_shift_0, d_shift_1, d_shift_2], 0)
    norm_sum = Sum(norm_terms.reshape(6, F, width // F).transpose(1, 0, 2), F32)
    norm_sum.start("fsdp", first_of["fsdp"], t3)
    cq_, ck, cv, ao = (
        Tall(left, right)
        for left, right in ((h_1_turned, dcq), (enc_turned, dek), (enc_turned, dev), (att_turned, da))
    )
    token = t3
    for one in (cq_, ck, cv, ao):
        token = one.start(token)
    qkv_shards = after(qkv_shards, token)
    qkv_shards.update(passed_on(qkv_shards))
    norm_sum.end(token)
    norm_sum.start("fsdp", rest_of["fsdp"], token)
    for one in (co, cq_, ck, cv, ao):
        token = one.start(token, fsdp_rest)
    mixed = after((unit_2 * gains[2] + shifts[2]).astype(BF), token)
    enc_term = dot_cols(after(dek, token), w_ckv[:, :width]) + dot_cols(dev, w_ckv[:, width:])
    enc_term = enc_term.astype(BF)
    d_att = to_columns([after(value, token, enc_term, qkv_shards) for value in d_att_got])

    d_att, part = lax.optimization_barrier((d_att, part))
    part = pair_sum_over(part, "ctx", 1)
    dq, dk, dv = attend_back(True, *self_in, d_att, att_t, att_lse, head_width, self_parts)
    dqkv_mine = jnp.concatenate([dq, dk, dv], 1)

    t5 = dqkv_mine
    w_qkv = place(
        width,
        [attn_qkv] + [after(qkv_shards[mask], t5) for mask in near + far],
        near_first(attn_qkv.shape[0]),
        f_scalar,
    )
    qkv = Tall(x_turned, dqkv_mine)
    token = qkv.start(t5)
    norm_sum.end(t5)
    norm_sum.start("seq", seq_bits, t5, "swap")
    dqkv = to_rows(dqkv_mine)
    gots = (co.got, cq_.got, ck.got, cv.got, ao.got)
    dqkv, w_qkv, gots, part = lax.optimization_barrier((dqkv, w_qkv, gots, part))
    for bit in rest_of["ctx"]:
        part = pair_sum_over(part, "ctx", bit)
    whole = lax.all_gather(part, "ctx", axis=0, tiled=True)
    for one, got in zip((co, cq_, ck, cv, ao), gots):
        one.got = got
        token = one.start(token)
    token = qkv.start(token, fsdp_rest)
    norm_sum.end(token)
    five = [one.end(token) for one in (co, cq_, ck, cv, ao)]
    t6 = (five, norm_sum.value, whole)

    piece_rows = five[0].shape[0] // C
    norm_flat = norm_sum.value.astype(BF).reshape(-1)
    norm_columns = -(-norm_flat.size // (128 * piece_rows)) * 128
    norm_flat = jnp.pad(norm_flat, (0, piece_rows * norm_columns - norm_flat.size))
    norm_flat = jnp.broadcast_to(norm_flat.reshape(1, piece_rows, norm_columns), (C, piece_rows, norm_columns))
    enc_columns = enc_rows * width // piece_rows
    terms = jnp.concatenate(
        [value.reshape(C, piece_rows, width) for value in five]
        + [enc_term.reshape(C, piece_rows, enc_columns), norm_flat],
        2,
    )
    terms, whole = lax.optimization_barrier((terms, whole))
    whole = lax.all_gather(whole, "seq", axis=0, tiled=True)
    terms_got = exchanged(lambda owner: pick(terms, owner), "ctx")
    token = qkv.start(t6)
    terms = sum((after(value, token).astype(F32) for value in terms_got[1:]), terms_got[0].astype(F32))
    qkv_part = qkv.end(terms)
    five = terms[:, : 5 * width].astype(BF)
    grad_encoder = terms[:, 5 * width : 5 * width + enc_columns].reshape(enc_rows, width)
    norm_sums = terms[:, 5 * width + enc_columns :].reshape(-1)[: 6 * width // F].reshape(6, width // F)
    t7 = (five, qkv_part)

    def share_over_ctx(value):
        return [value] + [swap(value, "ctx", mask) for mask in range(1, C)]

    def stacked(got):
        if got[0].shape[0] % 16 == 0:
            return place(C * got[0].shape[0], got, lambda c_ref: [
                (c_ref[0] ^ mask) * got[0].shape[0] for mask in range(C)
            ], c_scalar)
        return by_owner_of(got, "ctx").reshape(-1, got[0].shape[1])

    five, qkv_part = lax.optimization_barrier((five, qkv_part))
    five_got, qkv_got = share_over_ctx(five), share_over_ctx(qkv_part)
    dqkv = columns_in_order([after(value, t7) for value in dqkv], 3)
    grad_input = d_r1 + dot_cols(dqkv, w_qkv)
    five = stacked([after(value, grad_input) for value in five_got])
    qkv_part = stacked([after(value, grad_input) for value in qkv_got])
    t8 = (five, qkv_part)

    five, qkv_part, whole = lax.optimization_barrier((five, qkv_part, whole))
    five_other, qkv_other = swap(five, "seq", 1), swap(qkv_part, "seq", 1)
    whole = whole.reshape(S * C, tile_rows, width)
    grad_ff_out = whole[:, : tile_rows // 2].reshape(-1, width).astype(F32)
    strips = whole[:, tile_rows // 2 :].reshape(S * C, F, -1, ff_width)
    strips = exchanged(lambda owner: pick(strips, owner, 1).reshape(-1, ff_width), "fsdp")
    grad_ff_in = line_up(strips, 1, f_scalar, F32)
    widths = [width, width, 2 * width, width]
    grad_cross_out, grad_cross_q, grad_cross_kv, grad_attn_out = two_halves(
        functools.partial(split_columns_kernel, widths),
        five, five_other, s_scalar, [(five.shape[0], size) for size in widths],
    )
    if head_width % 128 == 0:
        (grad_attn_qkv,) = two_halves(
            functools.partial(spread_parts_kernel, C, 3),
            qkv_part, qkv_other, s_scalar, [(qkv_part.shape[0] // C, 3 * width)],
        )
    else:
        both = jnp.where(s == 0, jnp.stack([qkv_part, qkv_other]), jnp.stack([qkv_other, qkv_part]))
        both = both.reshape(2, C, -1, 3, head_width).transpose(0, 2, 3, 1, 4)
        grad_attn_qkv = both.reshape(-1, 3 * width).astype(F32)
    return (
        mixed.reshape(1, rows, width),
        grad_input.reshape(1, rows, width),
        grad_encoder.reshape(1, enc_rows, width),
        grad_attn_qkv, grad_attn_out, grad_cross_q, grad_cross_kv, grad_cross_out,
        grad_ff_in, grad_ff_out, norm_sums[:3], norm_sums[3:],
    )


def solution(mesh):
    rows = P(("seq", "fsdp"), "ctx", None)
    shard = P("fsdp", None)
    columns = P(None, "fsdp")
    return jax.shard_map(
        functools.partial(local, mesh.shape["seq"], mesh.shape["ctx"], mesh.shape["fsdp"]),
        mesh=mesh,
        in_specs=(rows, rows) + (shard,) * 7 + (columns, columns, P(), rows),
        out_specs=(rows, rows, rows) + (shard,) * 7 + (columns, columns),
        check_vma=False,
    )
```

```python
import functools

import jax
import jax.numpy as jnp
from jax import lax
from jax.experimental import pallas as pl
from jax.experimental.pallas import tpu as pltpu
from jax.sharding import PartitionSpec as P

HEADS = 16
HEAD_DIM = 64
TILE = 256
GROUP = 4
VMEM_LIMIT = 48 * 1024 * 1024
BF = jnp.bfloat16
F32 = jnp.float32
SMEM = pl.BlockSpec(memory_space=pltpu.SMEM)


def dot(left, right):
    return jnp.dot(left, right, preferred_element_type=F32)


def dot_rows(left, right):
    return lax.dot_general(left, right, (((0,), (0,)), ((), ())), preferred_element_type=F32)


def dot_cols(left, right):
    return lax.dot_general(left, right, (((1,), (1,)), ((), ())), preferred_element_type=F32)


def after(value, *others):
    return lax.optimization_barrier((value, *others))[0]


def causal_mask(tile):
    key = lax.broadcasted_iota(jnp.int32, (tile, tile), 0)
    query = lax.broadcasted_iota(jnp.int32, (tile, tile), 1)
    return key <= query


def lanes_of(heads):
    return [slice(head * HEAD_DIM, (head + 1) * HEAD_DIM) for head in range(heads)]


def joined_heads(values, axis):
    return values[0] if len(values) == 1 else jnp.concatenate(values, axis)


def spans(causal, at, keys):
    if not causal:
        return [(0, keys, False)]
    return ([(0, at * TILE, False)] if at else []) + [(at * TILE, TILE, True)]


def attend_kernel(causal, heads, steps, q_ref, k_ref, v_ref, out_ref, out_t_ref, lse_ref):
    query = q_ref[...] * HEAD_DIM**-0.5
    lanes = lanes_of(heads)

    def finish(outs):
        out_t = joined_heads(outs, 0)
        out_t_ref[...] = out_t
        out_ref[...] = out_t.T.astype(BF)

    def whole(at):
        parts = spans(causal, at, k_ref.shape[0])
        outs = []
        for head, lane in enumerate(lanes):
            scores = []
            for start, size, masked in parts:
                score = dot_cols(k_ref[start : start + size, lane], query[:, lane])
                scores.append(jnp.where(causal_mask(TILE), score, -1e30) if masked else score)
            top = functools.reduce(jnp.maximum, [jnp.max(score, 0, keepdims=True) for score in scores])
            probs = [jnp.exp(score - top) for score in scores]
            total = sum(jnp.sum(prob, 0, keepdims=True) for prob in probs)
            accum = sum(
                dot_rows(v_ref[start : start + size, lane], prob.astype(BF))
                for (start, size, _), prob in zip(parts, probs)
            )
            outs.append(accum / total)
            lse_ref[head : head + 1, :] = top + jnp.log(total)
        finish(outs)

    def rolled(at):
        def step(index, carry, masked):
            span = pl.ds(pl.multiple_of(index * TILE, TILE), TILE)
            keys, values = k_ref[span, :], v_ref[span, :]
            after_step = []
            for head, lane in enumerate(lanes):
                top, total, accum = carry[head]
                score = dot_cols(keys[:, lane], query[:, lane])
                if masked:
                    score = jnp.where(causal_mask(TILE), score, -1e30)
                new_top = jnp.maximum(top, jnp.max(score, 0, keepdims=True))
                prob = jnp.exp(score - new_top)
                decay = jnp.exp(top - new_top)
                total = total * decay + jnp.sum(prob, 0, keepdims=True)
                accum = accum * decay + dot_rows(values[:, lane], prob.astype(BF))
                after_step.append((new_top, total, accum))
            return tuple(after_step)

        rows = query.shape[0]
        carry = tuple(
            (
                jnp.full((1, rows), -1e30, F32),
                jnp.zeros((1, rows), F32),
                jnp.zeros((HEAD_DIM, rows), F32),
            )
            for _ in lanes
        )
        carry = lax.fori_loop(0, at, functools.partial(step, masked=False), carry)
        carry = step(at, carry, True)
        for head in range(heads):
            lse_ref[head : head + 1, :] = carry[head][0] + jnp.log(carry[head][1])
        finish([accum / total for _, total, accum in carry])

    run_tiles(causal, steps, whole, rolled)


def run_tiles(causal, steps, whole, rolled):
    at = pl.program_id(1)
    if not causal:
        whole(0)
    elif steps <= 4:
        for tile in range(steps):
            pl.when(at == tile)(functools.partial(whole, tile))
    else:
        rolled(at)


def attend_back_kernel(
    causal, heads, steps, q_ref, k_ref, v_ref, do_ref, out_t_ref, lse_ref,
    dq_ref, dk_ref, dv_ref, dk_sum, dv_sum,
):
    query = q_ref[...] * HEAD_DIM**-0.5
    d_out = do_ref[...]
    lanes = lanes_of(heads)
    weighed = d_out.astype(F32).T * out_t_ref[...]
    deltas = [jnp.sum(weighed[lane, :], 0, keepdims=True) for lane in lanes]
    totals = [lse_ref[head : head + 1, :] for head in range(heads)]

    @pl.when(pl.program_id(1) == 0)
    def _():
        dk_sum[...] = jnp.zeros_like(dk_sum)
        dv_sum[...] = jnp.zeros_like(dv_sum)

    def part(span, masked, d_query):
        keys, values = k_ref[span, :], v_ref[span, :]
        d_keys, d_values, out = [], [], []
        for head, lane in enumerate(lanes):
            score = dot_cols(keys[:, lane], query[:, lane])
            prob = jnp.exp(score - totals[head])
            if masked:
                prob = jnp.where(causal_mask(TILE), prob, 0.0)
            d_prob = dot_cols(values[:, lane], d_out[:, lane])
            d_score = (prob * (d_prob - deltas[head])).astype(BF)
            d_values.append(dot(prob.astype(BF), d_out[:, lane]))
            d_keys.append(dot(d_score, query[:, lane]))
            out.append(d_query[head] + dot_rows(keys[:, lane], d_score))
        dk_sum[span, :] += joined_heads(d_keys, 1)
        dv_sum[span, :] += joined_heads(d_values, 1)
        return tuple(out)

    start = tuple(jnp.zeros((HEAD_DIM, query.shape[0]), F32) for _ in lanes)

    def finish(d_query):
        dq_ref[...] = (joined_heads(d_query, 0).T * HEAD_DIM**-0.5).astype(BF)

    def whole(at):
        d_query = start
        for first, size, masked in spans(causal, at, k_ref.shape[0]):
            d_query = part(slice(first, first + size), masked, d_query)
        finish(d_query)

    def rolled(at):
        def step(index, carry):
            return part(pl.ds(pl.multiple_of(index * TILE, TILE), TILE), False, carry)

        d_query = lax.fori_loop(0, at, step, start)
        finish(part(pl.ds(pl.multiple_of(at * TILE, TILE), TILE), True, d_query))

    run_tiles(causal, steps, whole, rolled)

    @pl.when(pl.program_id(1) == steps - 1)
    def _():
        dk_ref[...] = dk_sum[...].astype(BF)
        dv_ref[...] = dv_sum[...].astype(BF)


def attend_specs(rows, keys, width, parts):
    group = min(width, GROUP * HEAD_DIM)
    groups = width // group

    def tall(part):
        return pl.BlockSpec((keys, group), lambda g, i: (0, part * groups + g))

    def query(part):
        return pl.BlockSpec((TILE, group), lambda g, i: (i, part * groups + g))

    return (
        (groups, rows // TILE), group, query(0), tall(parts[0]), tall(parts[1]), tall(0),
        pl.BlockSpec((group, TILE), lambda g, i: (g, i)),
        pl.BlockSpec((8, TILE), lambda g, i: (g, i)),
    )


def attend(causal, query, keys, values, width, parts):
    rows, depth = query.shape[0], keys.shape[0]
    grid, group, q_spec, k_spec, v_spec, _, t_spec, lse_spec = attend_specs(rows, depth, width, parts)
    return pl.pallas_call(
        functools.partial(attend_kernel, causal, group // HEAD_DIM, grid[1]),
        grid=grid,
        in_specs=[q_spec, k_spec, v_spec],
        out_specs=[q_spec, t_spec, lse_spec],
        out_shape=[
            jax.ShapeDtypeStruct((rows, width), BF),
            jax.ShapeDtypeStruct((width, rows), F32),
            jax.ShapeDtypeStruct((8 * grid[0], rows), F32),
        ],
        compiler_params=pltpu.CompilerParams(vmem_limit_bytes=VMEM_LIMIT),
        cost_estimate=pl.CostEstimate(
            flops=4 * rows * depth * width, bytes_accessed=8 * (rows + depth) * width,
            transcendentals=rows * depth * width // HEAD_DIM,
        ),
    )(query, keys, values)


def attend_back(causal, query, keys, values, d_out, out_t, lse, width, parts):
    rows, depth = query.shape[0], keys.shape[0]
    grid, group, q_spec, k_spec, v_spec, tall, t_spec, lse_spec = attend_specs(rows, depth, width, parts)
    return pl.pallas_call(
        functools.partial(attend_back_kernel, causal, group // HEAD_DIM, grid[1]),
        grid=grid,
        in_specs=[q_spec, k_spec, v_spec, q_spec, t_spec, lse_spec],
        out_specs=[q_spec, tall, tall],
        out_shape=[
            jax.ShapeDtypeStruct((rows, width), BF),
            jax.ShapeDtypeStruct((depth, width), BF),
            jax.ShapeDtypeStruct((depth, width), BF),
        ],
        scratch_shapes=[pltpu.VMEM((depth, group), F32), pltpu.VMEM((depth, group), F32)],
        compiler_params=pltpu.CompilerParams(vmem_limit_bytes=VMEM_LIMIT),
        cost_estimate=pl.CostEstimate(
            flops=10 * rows * depth * width, bytes_accessed=12 * (rows + depth) * width,
            transcendentals=rows * depth * width // HEAD_DIM,
        ),
    )(query, keys, values, d_out, out_t, lse)


IN_VMEM = pl.BlockSpec(memory_space=pltpu.VMEM)


def moved(kernel, scalars, values, out_shapes, dtype=BF):
    size = sum(value.size * value.dtype.itemsize for value in values)
    return pl.pallas_call(
        kernel,
        in_specs=[SMEM] * len(scalars) + [IN_VMEM] * len(values),
        out_specs=[IN_VMEM] * len(out_shapes),
        out_shape=[jax.ShapeDtypeStruct(shape, dtype) for shape in out_shapes],
        compiler_params=pltpu.CompilerParams(vmem_limit_bytes=VMEM_LIMIT),
        cost_estimate=pl.CostEstimate(flops=0, bytes_accessed=2 * size, transcendentals=0),
    )(*scalars, *values)


def place(rows, pieces, starts, *scalars):
    def kernel(*refs):
        values, out_ref = refs[len(scalars) : -1], refs[-1]
        for start, value in zip(starts(*refs[: len(scalars)]), values):
            out_ref[pl.ds(pl.multiple_of(start, 16), value.shape[0]), :] = value[...]

    return moved(kernel, scalars, pieces, [(rows, pieces[0].shape[1])])[0]


def cut(value, rows, count, starts, *scalars):
    def kernel(*refs):
        source, outs = refs[len(scalars)], refs[len(scalars) + 1 :]
        first = starts(*refs[: len(scalars)])
        size = rows // 2
        for index, start in enumerate(first):
            outs[index // 2][index % 2 * size : (index % 2 + 1) * size, :] = source[
                pl.ds(pl.multiple_of(start, 16), size), :
            ]

    return moved(kernel, scalars, [value], [(rows, value.shape[1])] * count)


def line_up(pieces, parts, at, dtype=BF):
    rows, columns = pieces[0].shape
    size = columns // parts

    def kernel(at_ref, *refs):
        values, out_ref = refs[:-1], refs[-1]
        for mask, value in enumerate(values):
            owner = at_ref[0] ^ mask
            for part in range(parts):
                start = part * size * len(values) + owner * size
                out_ref[:, pl.ds(pl.multiple_of(start, 128), size)] = value[
                    :, part * size : (part + 1) * size
                ].astype(dtype)

    return moved(kernel, [at], pieces, [(rows, columns * len(pieces))], dtype)[0]


def turn(value, starts, *scalars):
    def kernel(*refs):
        source, out_ref = refs[len(scalars) :]
        first = starts(*refs[: len(scalars)])
        size = source.shape[1] // len(first)
        for index, start in enumerate(first):
            out_ref[:, index * size : (index + 1) * size] = source[
                :, pl.ds(pl.multiple_of(start, 128), size)
            ]

    return moved(kernel, scalars, [value], [value.shape])[0]


def two_halves(kernel, own, other, at, out_widths):
    rows = out_widths[0][0]

    def body(at_ref, own_ref, other_ref, *outs):
        here = pl.program_id(0) == at_ref[0]
        pl.when(here)(lambda: kernel(own_ref, *outs))
        pl.when(jnp.logical_not(here))(lambda: kernel(other_ref, *outs))

    whole = pl.BlockSpec(own.shape, lambda i: (0, 0))
    return pl.pallas_call(
        body,
        grid=(2,),
        in_specs=[SMEM, whole, whole],
        out_specs=[pl.BlockSpec((rows, width), lambda i: (i, 0)) for _, width in out_widths],
        out_shape=[jax.ShapeDtypeStruct((2 * rows, width), F32) for _, width in out_widths],
        compiler_params=pltpu.CompilerParams(vmem_limit_bytes=VMEM_LIMIT),
        cost_estimate=pl.CostEstimate(flops=0, bytes_accessed=12 * own.size, transcendentals=0),
    )(at, own, other)


def split_columns_kernel(widths, source, *outs):
    at = 0
    for width, out in zip(widths, outs):
        out[...] = source[:, at : at + width].astype(F32)
        at += width


def spread_parts_kernel(owners, parts, source, out):
    rows, size = out.shape[0], source.shape[1] // parts
    width = out.shape[1] // parts
    for owner in range(owners):
        for part in range(parts):
            out[:, part * width + owner * size : part * width + (owner + 1) * size] = source[
                owner * rows : (owner + 1) * rows, part * size : (part + 1) * size
            ].astype(F32)


def norm_parts(value):
    centre = jnp.mean(value, -1, keepdims=True)
    centred = value - centre
    spread = jnp.mean(centred * centred, -1, keepdims=True)
    scale = lax.rsqrt(spread + 1e-05)
    return centred * scale, scale


def norm_back(grad, unit, scale, gain):
    slope = grad * gain
    d_value = scale * (
        slope
        - jnp.mean(slope, -1, keepdims=True)
        - unit * jnp.mean(slope * unit, -1, keepdims=True)
    )
    return d_value, jnp.sum(grad * unit, 0, keepdims=True), jnp.sum(grad, 0, keepdims=True)


def local(
    S, C, F,
    hidden, encoder, attn_qkv, attn_out, cross_q, cross_kv, cross_out, ff_in, ff_out,
    norm_gains, norm_biases, block_table, out_grad,
):
    rows, width = hidden.shape[1:]
    enc_rows = encoder.shape[1]
    half = rows // 2
    K = 2
    Y = F // K
    head_width = width // C
    ff_width = ff_in.shape[1] // F
    s, c, f = (lax.axis_index(name).astype(jnp.uint32) for name in ("seq", "ctx", "fsdp"))
    index_of = {"seq": s, "ctx": c, "fsdp": f}
    size_of = {"seq": S, "ctx": C, "fsdp": F}
    s_scalar, c_scalar, f_scalar = (index.astype(jnp.int32).reshape(1) for index in (s, c, f))

    def pick(value, index, axis=0):
        return lax.dynamic_index_in_dim(value, index, axis, keepdims=False)

    def bits_of(axis):
        return [1 << i for i in range(size_of[axis].bit_length() - 1)]

    def swap(value, axis, mask):
        return lax.ppermute(value, axis, [(i, i ^ mask) for i in range(size_of[axis])])

    def is_low(axis, bit):
        return (index_of[axis] & bit) == 0

    def give(parts, axis, bit):
        view = parts.reshape(parts.shape[0] // 2, 2, *parts.shape[1:])
        mine = (index_of[axis] // bit) & 1
        return pick(view, mine, 1), swap(pick(view, mine ^ 1, 1), axis, bit)

    def double(value, got, axis, bit):
        both = jnp.where(
            is_low(axis, bit), jnp.stack([value, got], 1), jnp.stack([got, value], 1)
        )
        return both.reshape(2 * value.shape[0], *value.shape[1:])

    def gather_over(value, axis):
        value = value[None]
        for bit in reversed(bits_of(axis)):
            value = double(value, swap(value, axis, bit), axis, bit)
        return value

    def by_owner_of(got, axis):
        stacked = jnp.stack(got)
        for bit in bits_of(axis):
            view = stacked.reshape(size_of[axis] // (2 * bit), 2, bit, *stacked.shape[1:])
            view = jnp.where(is_low(axis, bit), view, view[:, ::-1])
            stacked = view.reshape(stacked.shape)
        return stacked

    def exchanged(piece_of, axis):
        index = index_of[axis]
        return [piece_of(index)] + [
            swap(piece_of(index ^ mask), axis, mask) for mask in range(1, size_of[axis])
        ]

    def my_columns(weight, parts):
        size = weight.shape[1] // parts
        return jnp.concatenate(
            [
                lax.dynamic_slice_in_dim(weight, part * size + c * head_width, head_width, 1)
                for part in range(parts)
            ],
            1,
        )

    def to_rows(value):
        def starts(c_ref, table_ref):
            return [table_ref[c_ref[0] ^ mask, b] * half for mask in range(C) for b in range(2)]

        pieces = cut(value, rows, C, starts, c_scalar, block_table)
        return [pieces[0]] + [swap(pieces[mask], "ctx", mask) for mask in range(1, C)]

    def columns_in_order(got, parts):
        size = got[0].shape[1] // parts
        if size % 128 == 0:
            return line_up(got, parts, c_scalar)
        view = by_owner_of(got, "ctx").reshape(C, got[0].shape[0], parts, size)
        return view.transpose(1, 2, 0, 3).reshape(got[0].shape[0], C * parts * size)

    def to_columns(got):
        pieces = [value[b * half : (b + 1) * half] for value in got for b in range(2)]

        def starts(c_ref, table_ref):
            return [table_ref[c_ref[0] ^ mask, b] * half for mask in range(C) for b in range(2)]

        return place(C * rows, pieces, starts, c_scalar, block_table)

    def joined(lefts, rights):
        return dot_rows(jnp.concatenate(lefts, 0), jnp.concatenate(rights, 0)).astype(BF)

    flat = hidden.reshape(rows, width)
    enc = encoder.reshape(enc_rows, width)
    near = list(range(1, K))
    far = [mask for mask in range(F) if mask >= K]

    def near_first(size):
        return lambda f_ref: [(f_ref[0] ^ mask) * size for mask in range(F)]

    def spread(value):
        got = {mask: swap(value, "fsdp", mask) for mask in near}
        got.update({mask: swap(value, "fsdp", mask) for mask in far if mask % K == 0})
        return got

    def passed_on(got):
        return {mask: swap(got[mask - mask % K], "fsdp", mask % K) for mask in far if mask % K}

    slice_here = my_columns(attn_qkv, 3)
    norms = jnp.concatenate([norm_gains, norm_biases], 0)
    x_moving = [flat[:half], flat[half:]]
    x_pieces = list(x_moving)
    seen = []
    for step in range(C - 1):
        sent = {"x": [lax.ppermute(v, "ctx", [(i, (i + 1) % C) for i in range(C)]) for v in x_moving]}
        if step == 0:
            sent["slices"] = spread(slice_here)
            sent["norms"] = swap(norms, "fsdp", F // 2)
        sent = lax.optimization_barrier(sent)
        x_moving = sent["x"]
        x_pieces += x_moving
        seen.append(x_moving[0])
        if step == 0:
            slices, norms_got = sent["slices"], sent["norms"]
            slices.update(passed_on(slices))
            norms = double(norms[None], norms_got[None], "fsdp", F // 2)
            for bit in reversed(bits_of("fsdp")[:-1]):
                norms = double(norms, swap(norms, "fsdp", bit), "fsdp", bit)
    outs = spread(after(attn_out, seen[0]))
    outs.update(passed_on(outs))
    size = attn_qkv.shape[0]
    w_mine = place(width, [slice_here] + [slices[mask] for mask in near + far], near_first(size), f_scalar)
    w_out = place(width, [attn_out] + [outs[mask] for mask in near + far], near_first(size), f_scalar)
    norms = norms.astype(F32).transpose(1, 0, 2).reshape(6, width)
    gains, shifts = norms[:3], norms[3:]

    def x_starts(c_ref, table_ref):
        return [table_ref[(c_ref[0] + C - hop) & (C - 1), b] * half for hop in range(C) for b in range(2)]

    x_all = place(C * rows, x_pieces, x_starts, c_scalar, block_table)

    def gather(shard):
        return lax.all_gather(shard, "fsdp", axis=0, tiled=True)

    w_ckv = gather(cross_kv)
    w_cq, w_co = gather(after(cross_q, seen[0])), gather(after(cross_out, seen[0]))
    ff_later = after(ff_in, x_moving[0])
    ff_pieces = exchanged(
        lambda owner: lax.dynamic_slice_in_dim(ff_later, owner * ff_width, ff_width, 1), "fsdp"
    )
    w_ff = ff_out

    turns = [0]
    for bit in reversed(bits_of("fsdp")):
        turns = turns + [turn | bit for turn in turns]

    def turned(value):
        size = value.shape[1] // (F * S)
        if size % 128 == 0:
            return turn(
                value,
                lambda f_ref, s_ref: [
                    (f_ref[0] ^ mask) * (S * size) + (s_ref[0] ^ there) * size
                    for mask in turns
                    for there in range(S)
                ],
                f_scalar,
                s_scalar,
            )
        blocks = []
        for mask in turns:
            for there in range(S):
                at = (f ^ mask) * (S * size) + (s ^ there) * size
                blocks.append(lax.dynamic_slice_in_dim(value, at, size, 1))
        return jnp.concatenate(blocks, 1)

    class Tall:
        levels = [("fsdp", bit) for bit in bits_of("fsdp")] + [("seq", bit) for bit in bits_of("seq")]

        def __init__(self, left, right):
            self.left, self.right, self.got = left, right, []
            self.size = left.shape[1]
            self.at = 0

        def term(self, start, stop, token):
            right, got = self.right, self.got
            if token is not None:
                right, got = lax.optimization_barrier((right, got, token))[:2]
            total = dot_rows(self.left[:, start:stop], right)
            for value in got:
                total = total + value[start:stop].astype(F32)
            return total.astype(BF)

        def start(self, token=None, count=1):
            for _ in range(count):
                axis, bit = self.levels[self.at]
                self.at += 1
                self.size //= 2
                sent = self.term(self.size, 2 * self.size, token)
                self.got.append(swap(sent, axis, bit))
            return sent

        def end(self, token=None):
            return self.term(0, self.size, token)

    enc_all = after(enc, x_moving[0])[None]
    for bit in reversed(bits_of("ctx")):
        enc_some, enc_all = enc_all, double(enc_all, swap(enc_all, "ctx", bit), "ctx", bit)
    enc_all = enc_all.reshape(C * enc_rows, width)
    qkv = after(dot(x_all, w_mine).astype(BF), enc_some)
    if head_width % (2 * HEAD_DIM) == 0:
        self_in, self_parts = (qkv, qkv, qkv), (1, 2)
    else:
        self_in, self_parts = jnp.split(qkv, 3, 1), (0, 0)
    att_mine, att_t, att_lse = attend(True, *self_in, head_width, self_parts)
    att = columns_in_order(to_rows(att_mine), 1)
    ekv = dot(enc_all, w_ckv).astype(BF)
    w_in = place(width, ff_pieces, near_first(size), f_scalar)
    unit_0, scale_0 = norm_parts(flat.astype(F32) + dot(att, w_out))
    h_1 = unit_0 * gains[0] + shifts[0]
    h_1_low = h_1.astype(BF)

    cq = dot(h_1_low, w_cq).astype(BF)
    cat, cat_t, cat_lse = attend(False, cq, ekv, ekv, width, (0, 1))
    unit_1, scale_1 = norm_parts(h_1 + dot(cat, w_co))
    h_2 = unit_1 * gains[1] + shifts[1]
    h_2_low = h_2.astype(BF)

    def exchange(value, work, close):
        moving = {dy: swap(value, "fsdp", dy * K) for dy in range(1, Y)}

        def with_pair(there):
            return jnp.concatenate([there] + [swap(there, "fsdp", mask) for mask in near], 0)

        def pair_sum(term):
            view = term.astype(BF).reshape(K, -1, term.shape[1])
            total = view[0].astype(F32)
            for mask in near:
                total = total + swap(view[mask], "fsdp", mask).astype(F32)
            return total

        group = [with_pair(value)]
        worked = [work(0, group[0])]
        last = worked[0][0]
        for dy in range(1, Y):
            group.append(with_pair(after(moving[dy], last)))
            worked.append(work(dy, group[dy]))
            last = worked[dy][0]
        back, sent = [], None
        for dy in range(1, Y):
            sent = pair_sum(close(worked[dy])).astype(BF)
            back.append(swap(sent, "fsdp", dy * K))

        def finish(hold=()):
            own = worked[0] if sent is None else lax.optimization_barrier((worked[0], sent))[0]
            own = pair_sum(close(own))
            got = lax.optimization_barrier((back, own, hold))[0] if back else back
            return sum((value.astype(F32) for value in got), own)

        return group, worked, sent if back else last, finish

    def feed_forward(dy, value):
        pre = dot(value, w_in)
        cdf = 0.5 * (1.0 + lax.erf(pre * 0.5**0.5))
        slope = cdf + pre * (jnp.exp(-0.5 * pre * pre) * (2.0 * jnp.pi) ** -0.5)
        return lax.optimization_barrier(((pre * cdf).astype(BF), slope))

    h_2_rows, worked, _, finish = exchange(h_2_low, feed_forward, lambda got: dot(got[0], w_ff))
    acts, slopes = [got[0] for got in worked], [got[1] for got in worked]
    x_later, enc_later, w_out_later = (after(value, h_2_low) for value in (x_all, enc_all, w_out))
    x_turned, enc_turned = turned(x_later), turned(enc_later)
    cat_turned, h_1_turned, att_turned = turned(cat), turned(h_1_low), turned(after(att, h_2_low))
    w_out_turned = w_out_later.reshape(C, head_width, width)
    w_out_turned = [pick(w_out_turned, c ^ mask) for mask in range(C)]
    total = finish((x_turned, enc_turned, cat_turned, h_1_turned, att_turned, w_out_turned))
    unit_2, scale_2 = norm_parts(h_2 + total)

    grad = out_grad.reshape(rows, width).astype(F32)
    d_r3, d_gain_2, d_shift_2 = norm_back(grad, unit_2, scale_2, gains[2])

    def feed_back(dy, value):
        return ((dot_cols(value, w_ff) * slopes[dy]).astype(BF),)

    df_rows, worked, sent, finish = exchange(
        d_r3.astype(BF), feed_back, lambda got: dot_cols(got[0], w_in)
    )
    d_pres = [got[0] for got in worked]

    def by_owner(partial):
        return partial.astype(BF).reshape(F, -1, partial.shape[1])

    first_of = {axis: bits_of(axis)[:1] for axis in size_of}
    rest_of = {axis: bits_of(axis)[1:] for axis in size_of}

    class Sum:
        def __init__(self, parts, dtype=BF):
            self.value, self.pair, self.dtype = parts, None, dtype

        def start(self, axis, bits, token, kind="halve"):
            for at, bit in enumerate(bits):
                if at:
                    self.end()
                value = after(self.value, token)
                self.pair = give(value, axis, bit) if kind == "halve" else (value, swap(value, axis, bit))
                self.how = (kind, axis, bit)

        def end(self, token=None):
            if self.pair is None:
                return
            kept, got = self.pair
            self.pair = None
            if token is not None:
                got = after(got, token)
            if self.how[0] == "double":
                self.value = double(kept, got, *self.how[1:])
            else:
                self.value = (kept.astype(F32) + got.astype(F32)).astype(self.dtype)

        def shape(self, *shape):
            self.value = self.value.reshape(*shape)

    ctx_up, ctx_last = rest_of["ctx"][::-1], first_of["ctx"]
    seq_bits = bits_of("seq")

    tile_ff_in = joined([after(value, sent) for value in h_2_rows], d_pres)
    tile_ff_out = joined([after(act, sent) for act in acts], df_rows)
    tile_ff_in, tile_ff_out = lax.optimization_barrier((tile_ff_in, tile_ff_out))
    tiles = jnp.concatenate(
        [
            tile_ff_out.reshape(S * C, -1, width),
            tile_ff_in.reshape(F, S * C, -1, ff_width).transpose(1, 0, 2, 3).reshape(S * C, -1, width),
        ],
        1,
    )
    tile_rows = tiles.shape[1]
    d_h2 = d_r3 + finish((tiles,))

    part = lax.psum_scatter(tiles.reshape(-1, width), ("seq", "ctx"), scatter_dimension=0, tiled=True)

    qkv_shards = spread(after(attn_qkv, d_h2))
    d_r2, d_gain_1, d_shift_1 = norm_back(d_h2, unit_1, scale_1, gains[1])
    dc = d_r2.astype(BF)
    d_cat = dot_cols(dc, w_co).astype(BF)
    co = Tall(cat_turned, dc)
    token = co.start(d_cat)
    dcq, dek, dev = attend_back(False, cq, ekv, ekv, after(d_cat, token), cat_t, cat_lse, width, (0, 1))

    d_h1 = d_r2 + dot_cols(dcq, w_cq)
    d_r1, d_gain_0, d_shift_0 = norm_back(d_h1, unit_0, scale_0, gains[0])
    da = d_r1.astype(BF)
    d_att_pieces = [dot_cols(da, piece).astype(BF) for piece in w_out_turned]

    d_att_got = [d_att_pieces[0]] + [swap(d_att_pieces[mask], "ctx", mask) for mask in range(1, C)]
    t3 = (d_att_pieces, d_att_got[1] if C > 1 else ())
    fsdp_rest = len(rest_of["fsdp"])
    def join_rows(*refs):
        for row, ref in enumerate(refs[:-1]):
            refs[-1][row : row + 1, :] = ref[...]

    norm_terms = [d_gain_0, d_gain_1, d_gain_2, d_shift_0, d_shift_1, d_shift_2]
    norm_terms = moved(join_rows, [], norm_terms, [(6, width)], F32)[0]
    norm_sum = Sum(norm_terms.reshape(6, F, width // F).transpose(1, 0, 2), F32)
    norm_sum.start("fsdp", first_of["fsdp"], t3)
    cq_, ck, cv, ao = (
        Tall(left, right)
        for left, right in ((h_1_turned, dcq), (enc_turned, dek), (enc_turned, dev), (att_turned, da))
    )
    token = t3
    for one in (cq_, ck, cv, ao):
        token = one.start(token)
    qkv_shards = after(qkv_shards, token)
    qkv_shards.update(passed_on(qkv_shards))
    norm_sum.end(token)
    norm_sum.start("fsdp", rest_of["fsdp"], token)
    for one in (co, cq_, ck, cv, ao):
        token = one.start(token, fsdp_rest)
    mixed = after((unit_2 * gains[2] + shifts[2]).astype(BF), token)
    enc_term = dot_cols(after(dek, token), w_ckv[:, :width]) + dot_cols(dev, w_ckv[:, width:])
    enc_term = enc_term.astype(BF)
    d_att = to_columns([after(value, token, enc_term, qkv_shards) for value in d_att_got])

    dq, dk, dv = attend_back(True, *self_in, d_att, att_t, att_lse, head_width, self_parts)
    dqkv_mine = jnp.concatenate([dq, dk, dv], 1)

    t5 = dqkv_mine
    w_qkv = place(
        width,
        [attn_qkv] + [after(qkv_shards[mask], t5) for mask in near + far],
        near_first(attn_qkv.shape[0]),
        f_scalar,
    )
    qkv = Tall(x_turned, dqkv_mine)
    token = qkv.start(t5)
    norm_sum.end(t5)
    norm_sum.start("seq", seq_bits, t5, "swap")
    dqkv = to_rows(dqkv_mine)
    gots = (co.got, cq_.got, ck.got, cv.got, ao.got)
    dqkv, w_qkv, gots, part = lax.optimization_barrier((dqkv, w_qkv, gots, part))
    whole = lax.all_gather(part, "ctx", axis=0, tiled=True)
    for one, got in zip((co, cq_, ck, cv, ao), gots):
        one.got = got
        token = one.start(token)
    token = qkv.start(token, fsdp_rest)
    norm_sum.end(token)
    five = [one.end(token) for one in (co, cq_, ck, cv, ao)]
    t6 = (five, norm_sum.value, whole)

    piece_rows = five[0].shape[0] // C
    norm_flat = norm_sum.value.astype(BF).reshape(-1)
    norm_columns = -(-norm_flat.size // (128 * piece_rows)) * 128
    norm_flat = jnp.pad(norm_flat, (0, piece_rows * norm_columns - norm_flat.size))
    norm_flat = jnp.broadcast_to(norm_flat.reshape(1, piece_rows, norm_columns), (C, piece_rows, norm_columns))
    enc_columns = enc_rows * width // piece_rows
    terms = jnp.concatenate(
        [value.reshape(C, piece_rows, width) for value in five]
        + [enc_term.reshape(C, piece_rows, enc_columns), norm_flat],
        2,
    )
    terms, whole = lax.optimization_barrier((terms, whole))
    whole = lax.all_gather(whole, "seq", axis=0, tiled=True)
    terms_got = exchanged(lambda owner: pick(terms, owner), "ctx")
    token = qkv.start(t6)
    terms = sum((after(value, token).astype(F32) for value in terms_got[1:]), terms_got[0].astype(F32))
    qkv_part = qkv.end(terms)
    five = terms[:, : 5 * width].astype(BF)
    grad_encoder = terms[:, 5 * width : 5 * width + enc_columns].reshape(enc_rows, width)
    norm_sums = terms[:, 5 * width + enc_columns :].reshape(-1)[: 6 * width // F].reshape(6, width // F)
    t7 = (five, qkv_part)

    def share_over_ctx(value):
        return [value] + [swap(value, "ctx", mask) for mask in range(1, C)]

    def stacked(got):
        if got[0].shape[0] % 16 == 0:
            return place(C * got[0].shape[0], got, lambda c_ref: [
                (c_ref[0] ^ mask) * got[0].shape[0] for mask in range(C)
            ], c_scalar)
        return by_owner_of(got, "ctx").reshape(-1, got[0].shape[1])

    five, qkv_part = lax.optimization_barrier((five, qkv_part))
    five_got, qkv_got = share_over_ctx(five), share_over_ctx(qkv_part)
    dqkv = columns_in_order([after(value, t7) for value in dqkv], 3)
    grad_input = d_r1 + dot_cols(dqkv, w_qkv)
    five = stacked([after(value, grad_input) for value in five_got])
    qkv_part = stacked([after(value, grad_input) for value in qkv_got])
    t8 = (five, qkv_part)

    five, qkv_part, whole = lax.optimization_barrier((five, qkv_part, whole))
    five_other, qkv_other = swap(five, "seq", 1), swap(qkv_part, "seq", 1)
    whole = whole.reshape(S * C, tile_rows, width)
    grad_ff_out = whole[:, : tile_rows // 2].reshape(-1, width).astype(F32)
    strips = whole[:, tile_rows // 2 :].reshape(S * C, F, -1, ff_width)
    strips = exchanged(lambda owner: pick(strips, owner, 1).reshape(-1, ff_width), "fsdp")
    grad_ff_in = line_up(strips, 1, f_scalar, F32)
    widths = [width, width, 2 * width, width]
    grad_cross_out, grad_cross_q, grad_cross_kv, grad_attn_out = two_halves(
        functools.partial(split_columns_kernel, widths),
        five, five_other, s_scalar, [(five.shape[0], size) for size in widths],
    )
    if head_width % 128 == 0:
        (grad_attn_qkv,) = two_halves(
            functools.partial(spread_parts_kernel, C, 3),
            qkv_part, qkv_other, s_scalar, [(qkv_part.shape[0] // C, 3 * width)],
        )
    else:
        both = jnp.where(s == 0, jnp.stack([qkv_part, qkv_other]), jnp.stack([qkv_other, qkv_part]))
        both = both.reshape(2, C, -1, 3, head_width).transpose(0, 2, 3, 1, 4)
        grad_attn_qkv = both.reshape(-1, 3 * width).astype(F32)
    return (
        mixed.reshape(1, rows, width),
        grad_input.reshape(1, rows, width),
        grad_encoder.reshape(1, enc_rows, width),
        grad_attn_qkv, grad_attn_out, grad_cross_q, grad_cross_kv, grad_cross_out,
        grad_ff_in, grad_ff_out, norm_sums[:3], norm_sums[3:],
    )


def solution(mesh):
    rows = P(("seq", "fsdp"), "ctx", None)
    shard = P("fsdp", None)
    columns = P(None, "fsdp")
    return jax.shard_map(
        functools.partial(local, mesh.shape["seq"], mesh.shape["ctx"], mesh.shape["fsdp"]),
        mesh=mesh,
        in_specs=(rows, rows) + (shard,) * 7 + (columns, columns, P(), rows),
        out_specs=(rows, rows, rows) + (shard,) * 7 + (columns, columns),
        check_vma=False,
    )
```

```python
import functools

import jax
import jax.numpy as jnp
from jax import lax
from jax.experimental import pallas as pl
from jax.experimental.pallas import tpu as pltpu
from jax.sharding import PartitionSpec as P

HEADS = 16
HEAD_DIM = 64
TILE = 256
GROUP = 4
VMEM_LIMIT = 48 * 1024 * 1024
BF = jnp.bfloat16
F32 = jnp.float32
SMEM = pl.BlockSpec(memory_space=pltpu.SMEM)


def dot(left, right):
    return jnp.dot(left, right, preferred_element_type=F32)


def dot_rows(left, right):
    return lax.dot_general(left, right, (((0,), (0,)), ((), ())), preferred_element_type=F32)


def dot_cols(left, right):
    return lax.dot_general(left, right, (((1,), (1,)), ((), ())), preferred_element_type=F32)


def after(value, *others):
    return lax.optimization_barrier((value, *others))[0]


def causal_mask(tile):
    key = lax.broadcasted_iota(jnp.int32, (tile, tile), 0)
    query = lax.broadcasted_iota(jnp.int32, (tile, tile), 1)
    return key <= query


def lanes_of(heads):
    return [slice(head * HEAD_DIM, (head + 1) * HEAD_DIM) for head in range(heads)]


def joined_heads(values, axis):
    return values[0] if len(values) == 1 else jnp.concatenate(values, axis)


def spans(causal, at, keys):
    if not causal:
        return [(0, keys, False)]
    return ([(0, at * TILE, False)] if at else []) + [(at * TILE, TILE, True)]


def attend_kernel(causal, heads, steps, q_ref, k_ref, v_ref, out_ref, out_t_ref, lse_ref):
    query = q_ref[...] * HEAD_DIM**-0.5
    lanes = lanes_of(heads)

    def finish(outs):
        out_t = joined_heads(outs, 0)
        out_t_ref[...] = out_t
        out_ref[...] = out_t.T.astype(BF)

    def whole(at):
        parts = spans(causal, at, k_ref.shape[0])
        outs = []
        for head, lane in enumerate(lanes):
            scores = []
            for start, size, masked in parts:
                score = dot_cols(k_ref[start : start + size, lane], query[:, lane])
                scores.append(jnp.where(causal_mask(TILE), score, -1e30) if masked else score)
            top = functools.reduce(jnp.maximum, [jnp.max(score, 0, keepdims=True) for score in scores])
            probs = [jnp.exp(score - top) for score in scores]
            total = sum(jnp.sum(prob, 0, keepdims=True) for prob in probs)
            accum = sum(
                dot_rows(v_ref[start : start + size, lane], prob.astype(BF))
                for (start, size, _), prob in zip(parts, probs)
            )
            outs.append(accum / total)
            lse_ref[head : head + 1, :] = top + jnp.log(total)
        finish(outs)

    def rolled(at):
        def step(index, carry, masked):
            span = pl.ds(pl.multiple_of(index * TILE, TILE), TILE)
            keys, values = k_ref[span, :], v_ref[span, :]
            after_step = []
            for head, lane in enumerate(lanes):
                top, total, accum = carry[head]
                score = dot_cols(keys[:, lane], query[:, lane])
                if masked:
                    score = jnp.where(causal_mask(TILE), score, -1e30)
                new_top = jnp.maximum(top, jnp.max(score, 0, keepdims=True))
                prob = jnp.exp(score - new_top)
                decay = jnp.exp(top - new_top)
                total = total * decay + jnp.sum(prob, 0, keepdims=True)
                accum = accum * decay + dot_rows(values[:, lane], prob.astype(BF))
                after_step.append((new_top, total, accum))
            return tuple(after_step)

        rows = query.shape[0]
        carry = tuple(
            (
                jnp.full((1, rows), -1e30, F32),
                jnp.zeros((1, rows), F32),
                jnp.zeros((HEAD_DIM, rows), F32),
            )
            for _ in lanes
        )
        carry = lax.fori_loop(0, at, functools.partial(step, masked=False), carry)
        carry = step(at, carry, True)
        for head in range(heads):
            lse_ref[head : head + 1, :] = carry[head][0] + jnp.log(carry[head][1])
        finish([accum / total for _, total, accum in carry])

    run_tiles(causal, steps, whole, rolled)


def run_tiles(causal, steps, whole, rolled):
    at = pl.program_id(1)
    if not causal:
        whole(0)
    elif steps <= 4:
        for tile in range(steps):
            pl.when(at == tile)(functools.partial(whole, tile))
    else:
        rolled(at)


def attend_back_kernel(
    causal, heads, steps, q_ref, k_ref, v_ref, do_ref, out_t_ref, lse_ref,
    dq_ref, dk_ref, dv_ref, dk_sum, dv_sum,
):
    query = q_ref[...] * HEAD_DIM**-0.5
    d_out = do_ref[...]
    lanes = lanes_of(heads)
    weighed = d_out.astype(F32).T * out_t_ref[...]
    deltas = [jnp.sum(weighed[lane, :], 0, keepdims=True) for lane in lanes]
    totals = [lse_ref[head : head + 1, :] for head in range(heads)]

    @pl.when(pl.program_id(1) == 0)
    def _():
        dk_sum[...] = jnp.zeros_like(dk_sum)
        dv_sum[...] = jnp.zeros_like(dv_sum)

    def part(span, masked, d_query):
        keys, values = k_ref[span, :], v_ref[span, :]
        d_keys, d_values, out = [], [], []
        for head, lane in enumerate(lanes):
            score = dot_cols(keys[:, lane], query[:, lane])
            prob = jnp.exp(score - totals[head])
            if masked:
                prob = jnp.where(causal_mask(TILE), prob, 0.0)
            d_prob = dot_cols(values[:, lane], d_out[:, lane])
            d_score = (prob * (d_prob - deltas[head])).astype(BF)
            d_values.append(dot(prob.astype(BF), d_out[:, lane]))
            d_keys.append(dot(d_score, query[:, lane]))
            out.append(d_query[head] + dot_rows(keys[:, lane], d_score))
        dk_sum[span, :] += joined_heads(d_keys, 1)
        dv_sum[span, :] += joined_heads(d_values, 1)
        return tuple(out)

    start = tuple(jnp.zeros((HEAD_DIM, query.shape[0]), F32) for _ in lanes)

    def finish(d_query):
        dq_ref[...] = (joined_heads(d_query, 0).T * HEAD_DIM**-0.5).astype(BF)

    def whole(at):
        d_query = start
        for first, size, masked in spans(causal, at, k_ref.shape[0]):
            d_query = part(slice(first, first + size), masked, d_query)
        finish(d_query)

    def rolled(at):
        def step(index, carry):
            return part(pl.ds(pl.multiple_of(index * TILE, TILE), TILE), False, carry)

        d_query = lax.fori_loop(0, at, step, start)
        finish(part(pl.ds(pl.multiple_of(at * TILE, TILE), TILE), True, d_query))

    run_tiles(causal, steps, whole, rolled)

    @pl.when(pl.program_id(1) == steps - 1)
    def _():
        dk_ref[...] = dk_sum[...].astype(BF)
        dv_ref[...] = dv_sum[...].astype(BF)


def attend_specs(rows, keys, width, parts):
    group = min(width, GROUP * HEAD_DIM)
    groups = width // group

    def tall(part):
        return pl.BlockSpec((keys, group), lambda g, i: (0, part * groups + g))

    def query(part):
        return pl.BlockSpec((TILE, group), lambda g, i: (i, part * groups + g))

    return (
        (groups, rows // TILE), group, query(0), tall(parts[0]), tall(parts[1]), tall(0),
        pl.BlockSpec((group, TILE), lambda g, i: (g, i)),
        pl.BlockSpec((8, TILE), lambda g, i: (g, i)),
    )


def attend(causal, query, keys, values, width, parts):
    rows, depth = query.shape[0], keys.shape[0]
    grid, group, q_spec, k_spec, v_spec, _, t_spec, lse_spec = attend_specs(rows, depth, width, parts)
    return pl.pallas_call(
        functools.partial(attend_kernel, causal, group // HEAD_DIM, grid[1]),
        grid=grid,
        in_specs=[q_spec, k_spec, v_spec],
        out_specs=[q_spec, t_spec, lse_spec],
        out_shape=[
            jax.ShapeDtypeStruct((rows, width), BF),
            jax.ShapeDtypeStruct((width, rows), F32),
            jax.ShapeDtypeStruct((8 * grid[0], rows), F32),
        ],
        compiler_params=pltpu.CompilerParams(vmem_limit_bytes=VMEM_LIMIT),
        cost_estimate=pl.CostEstimate(
            flops=4 * rows * depth * width, bytes_accessed=8 * (rows + depth) * width,
            transcendentals=rows * depth * width // HEAD_DIM,
        ),
    )(query, keys, values)


def attend_back(causal, query, keys, values, d_out, out_t, lse, width, parts):
    rows, depth = query.shape[0], keys.shape[0]
    grid, group, q_spec, k_spec, v_spec, tall, t_spec, lse_spec = attend_specs(rows, depth, width, parts)
    return pl.pallas_call(
        functools.partial(attend_back_kernel, causal, group // HEAD_DIM, grid[1]),
        grid=grid,
        in_specs=[q_spec, k_spec, v_spec, q_spec, t_spec, lse_spec],
        out_specs=[q_spec, tall, tall],
        out_shape=[
            jax.ShapeDtypeStruct((rows, width), BF),
            jax.ShapeDtypeStruct((depth, width), BF),
            jax.ShapeDtypeStruct((depth, width), BF),
        ],
        scratch_shapes=[pltpu.VMEM((depth, group), F32), pltpu.VMEM((depth, group), F32)],
        compiler_params=pltpu.CompilerParams(vmem_limit_bytes=VMEM_LIMIT),
        cost_estimate=pl.CostEstimate(
            flops=10 * rows * depth * width, bytes_accessed=12 * (rows + depth) * width,
            transcendentals=rows * depth * width // HEAD_DIM,
        ),
    )(query, keys, values, d_out, out_t, lse)


IN_VMEM = pl.BlockSpec(memory_space=pltpu.VMEM)


def moved(kernel, scalars, values, out_shapes, dtype=BF):
    size = sum(value.size * value.dtype.itemsize for value in values)
    return pl.pallas_call(
        kernel,
        in_specs=[SMEM] * len(scalars) + [IN_VMEM] * len(values),
        out_specs=[IN_VMEM] * len(out_shapes),
        out_shape=[jax.ShapeDtypeStruct(shape, dtype) for shape in out_shapes],
        compiler_params=pltpu.CompilerParams(vmem_limit_bytes=VMEM_LIMIT),
        cost_estimate=pl.CostEstimate(flops=0, bytes_accessed=2 * size, transcendentals=0),
    )(*scalars, *values)


def place(rows, pieces, starts, *scalars):
    def kernel(*refs):
        values, out_ref = refs[len(scalars) : -1], refs[-1]
        for start, value in zip(starts(*refs[: len(scalars)]), values):
            out_ref[pl.ds(pl.multiple_of(start, 16), value.shape[0]), :] = value[...]

    return moved(kernel, scalars, pieces, [(rows, pieces[0].shape[1])])[0]


def cut(value, rows, count, starts, *scalars):
    def kernel(*refs):
        source, outs = refs[len(scalars)], refs[len(scalars) + 1 :]
        first = starts(*refs[: len(scalars)])
        size = rows // 2
        for index, start in enumerate(first):
            outs[index // 2][index % 2 * size : (index % 2 + 1) * size, :] = source[
                pl.ds(pl.multiple_of(start, 16), size), :
            ]

    return moved(kernel, scalars, [value], [(rows, value.shape[1])] * count)


def line_up(pieces, parts, at, dtype=BF):
    rows, columns = pieces[0].shape
    size = columns // parts

    def kernel(at_ref, *refs):
        values, out_ref = refs[:-1], refs[-1]
        for mask, value in enumerate(values):
            owner = at_ref[0] ^ mask
            for part in range(parts):
                start = part * size * len(values) + owner * size
                out_ref[:, pl.ds(pl.multiple_of(start, 128), size)] = value[
                    :, part * size : (part + 1) * size
                ].astype(dtype)

    return moved(kernel, [at], pieces, [(rows, columns * len(pieces))], dtype)[0]


def turn(value, starts, *scalars):
    def kernel(*refs):
        source, out_ref = refs[len(scalars) :]
        first = starts(*refs[: len(scalars)])
        size = source.shape[1] // len(first)
        for index, start in enumerate(first):
            out_ref[:, index * size : (index + 1) * size] = source[
                :, pl.ds(pl.multiple_of(start, 128), size)
            ]

    return moved(kernel, scalars, [value], [value.shape])[0]


def two_halves(kernel, own, other, at, out_widths):
    rows = out_widths[0][0]

    def body(at_ref, own_ref, other_ref, *outs):
        here = pl.program_id(0) == at_ref[0]
        pl.when(here)(lambda: kernel(own_ref, *outs))
        pl.when(jnp.logical_not(here))(lambda: kernel(other_ref, *outs))

    whole = pl.BlockSpec(own.shape, lambda i: (0, 0))
    return pl.pallas_call(
        body,
        grid=(2,),
        in_specs=[SMEM, whole, whole],
        out_specs=[pl.BlockSpec((rows, width), lambda i: (i, 0)) for _, width in out_widths],
        out_shape=[jax.ShapeDtypeStruct((2 * rows, width), F32) for _, width in out_widths],
        compiler_params=pltpu.CompilerParams(vmem_limit_bytes=VMEM_LIMIT),
        cost_estimate=pl.CostEstimate(flops=0, bytes_accessed=12 * own.size, transcendentals=0),
    )(at, own, other)


def split_columns_kernel(widths, source, *outs):
    at = 0
    for width, out in zip(widths, outs):
        out[...] = source[:, at : at + width].astype(F32)
        at += width


def spread_parts_kernel(owners, parts, source, out):
    rows, size = out.shape[0], source.shape[1] // parts
    width = out.shape[1] // parts
    for owner in range(owners):
        for part in range(parts):
            out[:, part * width + owner * size : part * width + (owner + 1) * size] = source[
                owner * rows : (owner + 1) * rows, part * size : (part + 1) * size
            ].astype(F32)


def norm_parts(value):
    centre = jnp.mean(value, -1, keepdims=True)
    centred = value - centre
    spread = jnp.mean(centred * centred, -1, keepdims=True)
    scale = lax.rsqrt(spread + 1e-05)
    return centred * scale, scale


def norm_back(grad, unit, scale, gain):
    slope = grad * gain
    d_value = scale * (
        slope
        - jnp.mean(slope, -1, keepdims=True)
        - unit * jnp.mean(slope * unit, -1, keepdims=True)
    )
    return d_value, jnp.sum(grad * unit, 0, keepdims=True), jnp.sum(grad, 0, keepdims=True)


def local(
    S, C, F,
    hidden, encoder, attn_qkv, attn_out, cross_q, cross_kv, cross_out, ff_in, ff_out,
    norm_gains, norm_biases, block_table, out_grad,
):
    rows, width = hidden.shape[1:]
    enc_rows = encoder.shape[1]
    half = rows // 2
    K = 2
    Y = F // K
    head_width = width // C
    ff_width = ff_in.shape[1] // F
    s, c, f = (lax.axis_index(name).astype(jnp.uint32) for name in ("seq", "ctx", "fsdp"))
    index_of = {"seq": s, "ctx": c, "fsdp": f}
    size_of = {"seq": S, "ctx": C, "fsdp": F}
    s_scalar, c_scalar, f_scalar = (index.astype(jnp.int32).reshape(1) for index in (s, c, f))

    def pick(value, index, axis=0):
        return lax.dynamic_index_in_dim(value, index, axis, keepdims=False)

    def bits_of(axis):
        return [1 << i for i in range(size_of[axis].bit_length() - 1)]

    def swap(value, axis, mask):
        return lax.ppermute(value, axis, [(i, i ^ mask) for i in range(size_of[axis])])

    def is_low(axis, bit):
        return (index_of[axis] & bit) == 0

    def give(parts, axis, bit):
        view = parts.reshape(parts.shape[0] // 2, 2, *parts.shape[1:])
        mine = (index_of[axis] // bit) & 1
        return pick(view, mine, 1), swap(pick(view, mine ^ 1, 1), axis, bit)

    def double(value, got, axis, bit):
        both = jnp.where(
            is_low(axis, bit), jnp.stack([value, got], 1), jnp.stack([got, value], 1)
        )
        return both.reshape(2 * value.shape[0], *value.shape[1:])

    def gather_over(value, axis):
        value = value[None]
        for bit in reversed(bits_of(axis)):
            value = double(value, swap(value, axis, bit), axis, bit)
        return value

    def by_owner_of(got, axis):
        stacked = jnp.stack(got)
        for bit in bits_of(axis):
            view = stacked.reshape(size_of[axis] // (2 * bit), 2, bit, *stacked.shape[1:])
            view = jnp.where(is_low(axis, bit), view, view[:, ::-1])
            stacked = view.reshape(stacked.shape)
        return stacked

    def exchanged(piece_of, axis):
        index = index_of[axis]
        return [piece_of(index)] + [
            swap(piece_of(index ^ mask), axis, mask) for mask in range(1, size_of[axis])
        ]

    def my_columns(weight, parts):
        size = weight.shape[1] // parts
        return jnp.concatenate(
            [
                lax.dynamic_slice_in_dim(weight, part * size + c * head_width, head_width, 1)
                for part in range(parts)
            ],
            1,
        )

    def to_rows(value):
        def starts(c_ref, table_ref):
            return [table_ref[c_ref[0] ^ mask, b] * half for mask in range(C) for b in range(2)]

        pieces = cut(value, rows, C, starts, c_scalar, block_table)
        return [pieces[0]] + [swap(pieces[mask], "ctx", mask) for mask in range(1, C)]

    def columns_in_order(got, parts):
        size = got[0].shape[1] // parts
        if size % 128 == 0:
            return line_up(got, parts, c_scalar)
        view = by_owner_of(got, "ctx").reshape(C, got[0].shape[0], parts, size)
        return view.transpose(1, 2, 0, 3).reshape(got[0].shape[0], C * parts * size)

    def to_columns(got):
        pieces = [value[b * half : (b + 1) * half] for value in got for b in range(2)]

        def starts(c_ref, table_ref):
            return [table_ref[c_ref[0] ^ mask, b] * half for mask in range(C) for b in range(2)]

        return place(C * rows, pieces, starts, c_scalar, block_table)

    def joined(lefts, rights):
        return dot_rows(jnp.concatenate(lefts, 0), jnp.concatenate(rights, 0)).astype(BF)

    flat = hidden.reshape(rows, width)
    enc = encoder.reshape(enc_rows, width)
    near = list(range(1, K))
    far = [mask for mask in range(F) if mask >= K]

    def near_first(size):
        return lambda f_ref: [(f_ref[0] ^ mask) * size for mask in range(F)]

    def spread(value):
        got = {mask: swap(value, "fsdp", mask) for mask in near}
        got.update({mask: swap(value, "fsdp", mask) for mask in far if mask % K == 0})
        return got

    def passed_on(got):
        return {mask: swap(got[mask - mask % K], "fsdp", mask % K) for mask in far if mask % K}

    slice_here = my_columns(attn_qkv, 3)
    norms = jnp.concatenate([norm_gains, norm_biases], 0)
    x_moving = [flat[:half], flat[half:]]
    x_pieces = list(x_moving)
    seen = []
    for step in range(C - 1):
        sent = {"x": [lax.ppermute(v, "ctx", [(i, (i + 1) % C) for i in range(C)]) for v in x_moving]}
        if step == 0:
            sent["slices"] = spread(slice_here)
            sent["norms"] = swap(norms, "fsdp", F // 2)
        sent = lax.optimization_barrier(sent)
        x_moving = sent["x"]
        x_pieces += x_moving
        seen.append(x_moving[0])
        if step == 0:
            slices, norms_got = sent["slices"], sent["norms"]
            slices.update(passed_on(slices))
            norms = double(norms[None], norms_got[None], "fsdp", F // 2)
            for bit in reversed(bits_of("fsdp")[:-1]):
                norms = double(norms, swap(norms, "fsdp", bit), "fsdp", bit)
    outs = spread(after(attn_out, seen[0]))
    outs.update(passed_on(outs))
    size = attn_qkv.shape[0]
    w_mine = place(width, [slice_here] + [slices[mask] for mask in near + far], near_first(size), f_scalar)
    w_out = place(width, [attn_out] + [outs[mask] for mask in near + far], near_first(size), f_scalar)
    norms = norms.astype(F32).transpose(1, 0, 2).reshape(6, width)
    gains, shifts = norms[:3], norms[3:]

    def x_starts(c_ref, table_ref):
        return [table_ref[(c_ref[0] + C - hop) & (C - 1), b] * half for hop in range(C) for b in range(2)]

    x_all = place(C * rows, x_pieces, x_starts, c_scalar, block_table)

    def gather(shard):
        return lax.all_gather(shard, "fsdp", axis=0, tiled=True)

    w_ckv = gather(cross_kv)
    w_cq, w_co = gather(cross_q), gather(after(cross_out, seen[0]))
    ff_later = after(ff_in, x_moving[0])
    ff_pieces = exchanged(
        lambda owner: lax.dynamic_slice_in_dim(ff_later, owner * ff_width, ff_width, 1), "fsdp"
    )
    w_ff = ff_out

    turns = [0]
    for bit in reversed(bits_of("fsdp")):
        turns = turns + [turn | bit for turn in turns]

    def turned(value):
        size = value.shape[1] // (F * S)
        if size % 128 == 0:
            return turn(
                value,
                lambda f_ref, s_ref: [
                    (f_ref[0] ^ mask) * (S * size) + (s_ref[0] ^ there) * size
                    for mask in turns
                    for there in range(S)
                ],
                f_scalar,
                s_scalar,
            )
        blocks = []
        for mask in turns:
            for there in range(S):
                at = (f ^ mask) * (S * size) + (s ^ there) * size
                blocks.append(lax.dynamic_slice_in_dim(value, at, size, 1))
        return jnp.concatenate(blocks, 1)

    class Tall:
        levels = [("fsdp", bit) for bit in bits_of("fsdp")] + [("seq", bit) for bit in bits_of("seq")]

        def __init__(self, left, right):
            self.left, self.right, self.got = left, right, []
            self.size = left.shape[1]
            self.at = 0

        def term(self, start, stop, token):
            right, got = self.right, self.got
            if token is not None:
                right, got = lax.optimization_barrier((right, got, token))[:2]
            total = dot_rows(self.left[:, start:stop], right)
            for value in got:
                total = total + value[start:stop].astype(F32)
            return total.astype(BF)

        def start(self, token=None, count=1):
            for _ in range(count):
                axis, bit = self.levels[self.at]
                self.at += 1
                self.size //= 2
                sent = self.term(self.size, 2 * self.size, token)
                self.got.append(swap(sent, axis, bit))
            return sent

        def end(self, token=None):
            return self.term(0, self.size, token)

    enc_all = after(enc, x_moving[0])[None]
    for bit in reversed(bits_of("ctx")):
        enc_some, enc_all = enc_all, double(enc_all, swap(enc_all, "ctx", bit), "ctx", bit)
    enc_all = enc_all.reshape(C * enc_rows, width)
    qkv = after(dot(x_all, w_mine).astype(BF), enc_some)
    if head_width % (2 * HEAD_DIM) == 0:
        self_in, self_parts = (qkv, qkv, qkv), (1, 2)
    else:
        self_in, self_parts = jnp.split(qkv, 3, 1), (0, 0)
    att_mine, att_t, att_lse = attend(True, *self_in, head_width, self_parts)
    att = columns_in_order(to_rows(att_mine), 1)
    ekv = dot(enc_all, w_ckv).astype(BF)
    w_in = place(width, ff_pieces, near_first(size), f_scalar)
    unit_0, scale_0 = norm_parts(flat.astype(F32) + dot(att, w_out))
    h_1 = unit_0 * gains[0] + shifts[0]
    h_1_low = h_1.astype(BF)

    cq = dot(h_1_low, w_cq).astype(BF)
    cat, cat_t, cat_lse = attend(False, cq, ekv, ekv, width, (0, 1))
    unit_1, scale_1 = norm_parts(h_1 + dot(cat, w_co))
    h_2 = unit_1 * gains[1] + shifts[1]
    h_2_low = h_2.astype(BF)

    def exchange(value, work, close):
        moving = {dy: swap(value, "fsdp", dy * K) for dy in range(1, Y)}

        def with_pair(there):
            return jnp.concatenate([there] + [swap(there, "fsdp", mask) for mask in near], 0)

        def pair_sum(term):
            view = term.astype(BF).reshape(K, -1, term.shape[1])
            total = view[0].astype(F32)
            for mask in near:
                total = total + swap(view[mask], "fsdp", mask).astype(F32)
            return total

        group = [with_pair(value)]
        worked = [work(0, group[0])]
        last = worked[0][0]
        for dy in range(1, Y):
            group.append(with_pair(after(moving[dy], last)))
            worked.append(work(dy, group[dy]))
            last = worked[dy][0]
        back, sent = [], None
        for dy in range(1, Y):
            sent = pair_sum(close(worked[dy])).astype(BF)
            back.append(swap(sent, "fsdp", dy * K))

        def finish(hold=()):
            own = worked[0] if sent is None else lax.optimization_barrier((worked[0], sent))[0]
            own = pair_sum(close(own))
            got = lax.optimization_barrier((back, own, hold))[0] if back else back
            return sum((value.astype(F32) for value in got), own)

        return group, worked, sent if back else last, finish

    def feed_forward(dy, value):
        pre = dot(value, w_in)
        cdf = 0.5 * (1.0 + lax.erf(pre * 0.5**0.5))
        slope = cdf + pre * (jnp.exp(-0.5 * pre * pre) * (2.0 * jnp.pi) ** -0.5)
        return lax.optimization_barrier(((pre * cdf).astype(BF), slope))

    h_2_rows, worked, _, finish = exchange(h_2_low, feed_forward, lambda got: dot(got[0], w_ff))
    acts, slopes = [got[0] for got in worked], [got[1] for got in worked]
    x_later, enc_later, w_out_later = (after(value, h_2_low) for value in (x_all, enc_all, w_out))
    x_turned, enc_turned = turned(x_later), turned(enc_later)
    cat_turned, h_1_turned, att_turned = turned(cat), turned(h_1_low), turned(after(att, h_2_low))
    w_out_turned = w_out_later.reshape(C, head_width, width)
    w_out_turned = [pick(w_out_turned, c ^ mask) for mask in range(C)]
    total = finish((x_turned, enc_turned, cat_turned, h_1_turned, att_turned, w_out_turned))
    unit_2, scale_2 = norm_parts(h_2 + total)

    grad = out_grad.reshape(rows, width).astype(F32)
    d_r3, d_gain_2, d_shift_2 = norm_back(grad, unit_2, scale_2, gains[2])

    def feed_back(dy, value):
        return ((dot_cols(value, w_ff) * slopes[dy]).astype(BF),)

    df_rows, worked, sent, finish = exchange(
        d_r3.astype(BF), feed_back, lambda got: dot_cols(got[0], w_in)
    )
    d_pres = [got[0] for got in worked]

    def by_owner(partial):
        return partial.astype(BF).reshape(F, -1, partial.shape[1])

    first_of = {axis: bits_of(axis)[:1] for axis in size_of}
    rest_of = {axis: bits_of(axis)[1:] for axis in size_of}

    class Sum:
        def __init__(self, parts, dtype=BF):
            self.value, self.pair, self.dtype = parts, None, dtype

        def start(self, axis, bits, token, kind="halve"):
            for at, bit in enumerate(bits):
                if at:
                    self.end()
                value = after(self.value, token)
                self.pair = give(value, axis, bit) if kind == "halve" else (value, swap(value, axis, bit))
                self.how = (kind, axis, bit)

        def end(self, token=None):
            if self.pair is None:
                return
            kept, got = self.pair
            self.pair = None
            if token is not None:
                got = after(got, token)
            if self.how[0] == "double":
                self.value = double(kept, got, *self.how[1:])
            else:
                self.value = (kept.astype(F32) + got.astype(F32)).astype(self.dtype)

        def shape(self, *shape):
            self.value = self.value.reshape(*shape)

    ctx_up, ctx_last = rest_of["ctx"][::-1], first_of["ctx"]
    seq_bits = bits_of("seq")

    tile_ff_in = joined([after(value, sent) for value in h_2_rows], d_pres)
    tile_ff_out = joined([after(act, sent) for act in acts], df_rows)
    tile_ff_in, tile_ff_out = lax.optimization_barrier((tile_ff_in, tile_ff_out))
    tiles = jnp.concatenate(
        [
            tile_ff_out.reshape(S * C, -1, width),
            tile_ff_in.reshape(F, S * C, -1, ff_width).transpose(1, 0, 2, 3).reshape(S * C, -1, width),
        ],
        1,
    )
    tile_rows = tiles.shape[1]
    d_h2 = d_r3 + finish((tiles,))

    part = lax.psum_scatter(tiles.reshape(-1, width), ("seq", "ctx"), scatter_dimension=0, tiled=True)

    qkv_shards = spread(after(attn_qkv, d_h2))
    d_r2, d_gain_1, d_shift_1 = norm_back(d_h2, unit_1, scale_1, gains[1])
    dc = d_r2.astype(BF)
    d_cat = dot_cols(dc, w_co).astype(BF)
    co = Tall(cat_turned, dc)
    token = co.start(d_cat)
    dcq, dek, dev = attend_back(False, cq, ekv, ekv, after(d_cat, token), cat_t, cat_lse, width, (0, 1))

    d_h1 = d_r2 + dot_cols(dcq, w_cq)
    d_r1, d_gain_0, d_shift_0 = norm_back(d_h1, unit_0, scale_0, gains[0])
    da = d_r1.astype(BF)
    d_att_pieces = [dot_cols(da, piece).astype(BF) for piece in w_out_turned]

    d_att_got = [d_att_pieces[0]] + [swap(d_att_pieces[mask], "ctx", mask) for mask in range(1, C)]
    t3 = (d_att_pieces, d_att_got[1] if C > 1 else ())
    fsdp_rest = len(rest_of["fsdp"])
    def join_rows(*refs):
        for row, ref in enumerate(refs[:-1]):
            refs[-1][row : row + 1, :] = ref[...]

    norm_terms = [d_gain_0, d_gain_1, d_gain_2, d_shift_0, d_shift_1, d_shift_2]
    norm_terms = moved(join_rows, [], norm_terms, [(6, width)], F32)[0]
    norm_sum = Sum(norm_terms.reshape(6, F, width // F).transpose(1, 0, 2), F32)
    norm_sum.start("fsdp", first_of["fsdp"], t3)
    cq_, ck, cv, ao = (
        Tall(left, right)
        for left, right in ((h_1_turned, dcq), (enc_turned, dek), (enc_turned, dev), (att_turned, da))
    )
    token = t3
    for one in (cq_, ck, cv, ao):
        token = one.start(token)
    qkv_shards = after(qkv_shards, token)
    qkv_shards.update(passed_on(qkv_shards))
    norm_sum.end(token)
    norm_sum.start("fsdp", rest_of["fsdp"], token)
    for one in (co, cq_, ck, cv, ao):
        token = one.start(token, fsdp_rest)
    mixed = after((unit_2 * gains[2] + shifts[2]).astype(BF), token)
    enc_term = dot_cols(after(dek, token), w_ckv[:, :width]) + dot_cols(dev, w_ckv[:, width:])
    enc_term = enc_term.astype(BF)
    d_att = to_columns([after(value, token, enc_term, qkv_shards) for value in d_att_got])

    dq, dk, dv = attend_back(True, *self_in, d_att, att_t, att_lse, head_width, self_parts)
    dqkv_mine = jnp.concatenate([dq, dk, dv], 1)

    t5 = dqkv_mine
    w_qkv = place(
        width,
        [attn_qkv] + [after(qkv_shards[mask], t5) for mask in near + far],
        near_first(attn_qkv.shape[0]),
        f_scalar,
    )
    qkv = Tall(x_turned, dqkv_mine)
    token = qkv.start(t5)
    norm_sum.end(t5)
    norm_sum.start("seq", seq_bits, t5, "swap")
    dqkv = to_rows(dqkv_mine)
    gots = (co.got, cq_.got, ck.got, cv.got, ao.got)
    dqkv, w_qkv, gots, part = lax.optimization_barrier((dqkv, w_qkv, gots, part))
    whole = lax.all_gather(part, "ctx", axis=0, tiled=True)
    for one, got in zip((co, cq_, ck, cv, ao), gots):
        one.got = got
        token = one.start(token)
    token = qkv.start(token, fsdp_rest)
    norm_sum.end(token)
    five = [one.end(token) for one in (co, cq_, ck, cv, ao)]
    t6 = (five, norm_sum.value, whole)

    piece_rows = five[0].shape[0] // C
    norm_flat = norm_sum.value.astype(BF).reshape(-1)
    norm_columns = -(-norm_flat.size // (128 * piece_rows)) * 128
    norm_flat = jnp.pad(norm_flat, (0, piece_rows * norm_columns - norm_flat.size))
    norm_flat = jnp.broadcast_to(norm_flat.reshape(1, piece_rows, norm_columns), (C, piece_rows, norm_columns))
    enc_columns = enc_rows * width // piece_rows
    terms = jnp.concatenate(
        [value.reshape(C, piece_rows, width) for value in five]
        + [enc_term.reshape(C, piece_rows, enc_columns), norm_flat],
        2,
    )
    terms, whole = lax.optimization_barrier((terms, whole))
    whole = lax.all_gather(whole, "seq", axis=0, tiled=True)
    terms_got = exchanged(lambda owner: pick(terms, owner), "ctx")
    token = qkv.start(t6)
    terms = sum((after(value, token).astype(F32) for value in terms_got[1:]), terms_got[0].astype(F32))
    qkv_part = qkv.end(terms)
    five = terms[:, : 5 * width].astype(BF)
    grad_encoder = terms[:, 5 * width : 5 * width + enc_columns].reshape(enc_rows, width)
    norm_sums = terms[:, 5 * width + enc_columns :].reshape(-1)[: 6 * width // F].reshape(6, width // F)
    t7 = (five, qkv_part)

    def share_over_ctx(value):
        return [value] + [swap(value, "ctx", mask) for mask in range(1, C)]

    def stacked(got):
        if got[0].shape[0] % 16 == 0:
            return place(C * got[0].shape[0], got, lambda c_ref: [
                (c_ref[0] ^ mask) * got[0].shape[0] for mask in range(C)
            ], c_scalar)
        return by_owner_of(got, "ctx").reshape(-1, got[0].shape[1])

    five, qkv_part = lax.optimization_barrier((five, qkv_part))
    five_got, qkv_got = share_over_ctx(five), share_over_ctx(qkv_part)
    dqkv = columns_in_order([after(value, t7) for value in dqkv], 3)
    grad_input = d_r1 + dot_cols(dqkv, w_qkv)
    five = stacked([after(value, grad_input) for value in five_got])
    qkv_part = stacked([after(value, grad_input) for value in qkv_got])
    t8 = (five, qkv_part)

    five, qkv_part, whole = lax.optimization_barrier((five, qkv_part, whole))
    five_other, qkv_other = swap(five, "seq", 1), swap(qkv_part, "seq", 1)
    whole = whole.reshape(S * C, tile_rows, width)
    grad_ff_out = whole[:, : tile_rows // 2].reshape(-1, width).astype(F32)
    strips = whole[:, tile_rows // 2 :].reshape(S * C, F, -1, ff_width)
    strips = exchanged(lambda owner: pick(strips, owner, 1).reshape(-1, ff_width), "fsdp")
    grad_ff_in = line_up(strips, 1, f_scalar, F32)
    widths = [width, width, 2 * width, width]
    grad_cross_out, grad_cross_q, grad_cross_kv, grad_attn_out = two_halves(
        functools.partial(split_columns_kernel, widths),
        five, five_other, s_scalar, [(five.shape[0], size) for size in widths],
    )
    if head_width % 128 == 0:
        (grad_attn_qkv,) = two_halves(
            functools.partial(spread_parts_kernel, C, 3),
            qkv_part, qkv_other, s_scalar, [(qkv_part.shape[0] // C, 3 * width)],
        )
    else:
        both = jnp.where(s == 0, jnp.stack([qkv_part, qkv_other]), jnp.stack([qkv_other, qkv_part]))
        both = both.reshape(2, C, -1, 3, head_width).transpose(0, 2, 3, 1, 4)
        grad_attn_qkv = both.reshape(-1, 3 * width).astype(F32)
    return (
        mixed.reshape(1, rows, width),
        grad_input.reshape(1, rows, width),
        grad_encoder.reshape(1, enc_rows, width),
        grad_attn_qkv, grad_attn_out, grad_cross_q, grad_cross_kv, grad_cross_out,
        grad_ff_in, grad_ff_out, norm_sums[:3], norm_sums[3:],
    )


def solution(mesh):
    rows = P(("seq", "fsdp"), "ctx", None)
    shard = P("fsdp", None)
    columns = P(None, "fsdp")
    return jax.shard_map(
        functools.partial(local, mesh.shape["seq"], mesh.shape["ctx"], mesh.shape["fsdp"]),
        mesh=mesh,
        in_specs=(rows, rows) + (shard,) * 7 + (columns, columns, P(), rows),
        out_specs=(rows, rows, rows) + (shard,) * 7 + (columns, columns),
        check_vma=False,
    )
```
